512 devices in a mesh: row: 16 (over z_lo, core), col: 32 (over y, x, z_hi).
Axes of the slice: x: 4, y: 4, z: 16 (z_hi: 2, z_lo: 8; z = z_hi * 8 + z_lo), core: 2. Of those that a mesh axis runs over, the one named last changes fastest.
Arguments:
- amplitudes: float32 [6144, 6144], P(('row', 'col')), may hold values from -6 to 6
- integrals: float32 [6144, 6144], P(('row', 'col')), may hold values from -0.078125 to 0.078125
- occupied_energy: float32 [150], replicated, may hold values from -1.5 to -0.3
- virtual_energy: float32 [1536], replicated, may hold values from 0.2 to 4
- window_i: int32 [4], replicated, may hold values from 0 to 149
- window_j: int32 [4], replicated, may hold values from 0 to 149
Outputs:
- update: float32 [6144, 6144], P(('row', 'col'))
The draws below stay inside these ranges and needn't reach their ends.
Inputs may be any that keep to these rules, and one draw needn't show every extreme that they name: `window_i`: indices of occupied orbitals. `window_j`: indices of occupied orbitals.
All inputs are finite; a program needn't handle non-finite values.
Results may differ from the reference program's by a relative error of at most 0.00007.
Values sent between devices are 32-bit elements; how exact they have to be, the bound alone decides.
No kernel may reach another device: no remote copies, remote signals or barrier semaphores. Data moves between devices by JAX's collectives and lax.ppermute only.
A program may use at most 128 MiB of HBM per device.

```python
import math
import jax
import jax.numpy as jnp
from jax import lax

VIRT = 1536
OCC_WIN = 4
NOCC = 150
ORDER = 6144


def plant(result, rng, least, high):
    place = [jax.random.randint(jax.random.fold_in(rng, axis), (), 0, length) for axis, length in enumerate(result.shape)]
    widest = result.shape.index(max(result.shape))
    neighbour = place[:widest] + [(place[widest] + 1) % result.shape[widest]] + place[widest + 1:]
    return result.at[tuple(place)].set(least).at[tuple(neighbour)].set(high)


def block_scale(rng, shape, shards, low, largest):
    def one(dim, blocks):
        heights = jax.random.uniform(jax.random.fold_in(jax.random.fold_in(rng, 6), dim), (blocks,), jnp.float32, low / len(shards), largest / len(shards))
        return jnp.repeat(jnp.exp(heights), shape[dim] // blocks).reshape((-1,) + (1,) * (len(shape) - dim - 1))

    level = one(*shards[0])
    for cut in shards[1:]:
        level = level * one(*cut)
    return level


def bell_draw(rng, dims, spread, reach, pieces=(), dtype=jnp.bfloat16):
    array = jax.random.normal(rng, dims, jnp.float32) * spread
    if len(pieces) > 0:
        array = block_scale(rng, dims, pieces, -0.22, 0.18) * array
    return jnp.clip(array, min=-reach, max=reach).astype(dtype)


def setup_inputs(seed: int = 0) -> dict:
    streams_of = jax.random.split(jax.random.key(seed), 7)
    return {
        "amplitudes": bell_draw(streams_of[0], (ORDER, ORDER), 1.0, 6.0, ((0, 512),), jnp.float32),
        "integrals": bell_draw(streams_of[1], (ORDER, ORDER), ORDER ** -0.5, 0.078125, ((0, 512),), jnp.float32),
        "occupied_energy": jnp.clip(jax.random.uniform(streams_of[2], (NOCC,), jnp.float32, -1.5, -0.3), -1.5, -0.3),
        "virtual_energy": jnp.clip(jnp.exp(jax.random.uniform(streams_of[3], (VIRT,), jnp.float32, math.log(0.2), math.log(4.0))), 0.2, 4.0),
        "window_i": plant(jax.random.randint(streams_of[4], (OCC_WIN,), 0, NOCC), jax.random.fold_in(streams_of[4], 1), 0, NOCC - 1).astype(jnp.int32),
        "window_j": plant(jax.random.randint(streams_of[5], (OCC_WIN,), 0, NOCC), jax.random.fold_in(streams_of[5], 1), 0, NOCC - 1).astype(jnp.int32),
    }


def reference(amplitudes, integrals, occupied_energy, virtual_energy, window_i, window_j):
    cycle = jnp.dot(amplitudes, integrals, precision=lax.Precision.HIGHEST, preferred_element_type=jnp.float32)
    row_shift = (occupied_energy[window_i][:, None] - virtual_energy[None, :]).reshape(-1)
    col_shift = (occupied_energy[window_j][:, None] - virtual_energy[None, :]).reshape(-1)
    return cycle / (row_shift[:, None] + col_shift[None, :])
```

```python
import jax
import jax.numpy as jnp
import numpy as np
from jax import lax
from jax.sharding import Mesh, PartitionSpec as P

AXES = ("zlo", "core", "y", "x", "zhi")
SIZES = (8, 2, 4, 4, 2)
PLANE = ("y", "x")
RING = ("zhi", "zlo")


def column_order():
    source = np.arange(768).reshape(2, 16, 2, 12).transpose(2, 0, 1, 3).reshape(-1)
    order = np.zeros((768, 768), np.float32)
    order[source, np.arange(768)] = 1.0
    return order


def per_device(amplitudes, integrals, occupied_energy, virtual_energy, window_i, window_j):
    rows = amplitudes.shape[0]
    blocks = integrals.reshape(rows, 16, 384).transpose(1, 0, 2)
    blocks = lax.all_to_all(blocks, PLANE, split_axis=0, concat_axis=0, tiled=True)
    panel = lax.all_gather(blocks.reshape(16 * rows, 384), RING, axis=0, tiled=True)
    pieces = amplitudes.reshape(rows, 4, 2, 2, 384).transpose(3, 0, 1, 2, 4)
    pieces = jnp.dot(
        pieces.reshape(-1, 768),
        jnp.asarray(column_order()),
        precision=lax.Precision.HIGHEST,
        preferred_element_type=jnp.float32,
    )
    pieces = pieces.reshape(2, rows, 4, 2, 384).transpose(0, 1, 3, 2, 4).reshape(2, rows, 3072)
    pieces = lax.all_to_all(pieces, "core", split_axis=0, concat_axis=0, tiled=True)
    pieces = pieces.reshape(1, 2 * rows, 3072)
    spread = jnp.broadcast_to(pieces, (16, 2 * rows, 3072))
    left = lax.all_to_all(spread, PLANE, split_axis=0, concat_axis=0, tiled=True)
    partial = jnp.dot(
        left.reshape(32 * rows, 3072),
        panel,
        precision=lax.Precision.HIGH,
        preferred_element_type=jnp.float32,
    )
    parts = lax.all_to_all(
        partial.reshape(32, rows, 384), ("y", "x", "core"), split_axis=0, concat_axis=0, tiled=True
    )
    stored = parts.reshape(16, 2, rows, 384).sum(1).transpose(1, 0, 2).reshape(rows, 6144)
    index = lax.axis_index(AXES)
    row_shift = (occupied_energy[window_i][:, None] - virtual_energy[None, :]).reshape(-1)
    col_shift = (occupied_energy[window_j][:, None] - virtual_energy[None, :]).reshape(-1)
    local_shift = lax.dynamic_slice_in_dim(row_shift, index * rows, rows, 0)
    return stored / (local_shift[:, None] + col_shift[None, :])


def solution(mesh):
    fine = Mesh(mesh.devices.reshape(SIZES), AXES)
    split = P(AXES, None)
    return jax.shard_map(
        per_device,
        mesh=fine,
        in_specs=(split, split, P(), P(), P(), P()),
        out_specs=split,
        check_vma=False,
    )
```

```python
import functools

import jax
import jax.numpy as jnp
import numpy as np
from jax import lax
from jax.experimental import pallas as pl
from jax.experimental.pallas import tpu as pltpu
from jax.sharding import Mesh, PartitionSpec as P

AXES = ("zlo", "core", "y", "x", "zhi")
SIZES = (8, 2, 4, 4, 2)
PLANE = ("y", "x")
RING = ("zhi", "zlo")
ROWS = 12
WIDE = 384
HALF = 3072
STEP = 512
VMEM = pl.BlockSpec(memory_space=pltpu.VMEM)


def params():
    return pltpu.CompilerParams(vmem_limit_bytes=48 * 1024 * 1024)


def cost(flops, moved):
    return pl.CostEstimate(flops=flops, bytes_accessed=moved, transcendentals=0)


def column_order():
    source = np.arange(768).reshape(2, 16, 2, 12).transpose(2, 0, 1, 3).reshape(-1)
    order = np.zeros((768, 768), np.float32)
    order[source, np.arange(768)] = 1
    return order


def prepare_kernel(core_ref, a_ref, b_ref, own_ref, other_ref, blocks_ref):
    core = core_ref[0]
    for z in range(8):
        at = slice(WIDE * z, WIDE * z + WIDE)
        own_ref[:, at] = a_ref[:, pl.ds(pl.multiple_of(768 * z + WIDE * core, 128), WIDE)]
        other_ref[:, at] = a_ref[:, pl.ds(pl.multiple_of(768 * z + WIDE - WIDE * core, 128), WIDE)]
    for i in range(16):
        blocks_ref[i] = b_ref[:, WIDE * i : WIDE * i + WIDE]


def spread_kernel(core_ref, own_ref, other_ref, order_ref, out_ref, rows_ref):
    first = core_ref[0] == 0
    own, other = own_ref[...], other_ref[...]
    upper, lower = jnp.where(first, own, other), jnp.where(first, other, own)
    order = order_ref[...].astype(jnp.bfloat16)
    for q in range(4):
        lanes = slice(768 * q, 768 * q + 768)
        x = jnp.concatenate([upper[:, lanes], lower[:, lanes]], axis=0)
        total = None
        for _ in range(3):
            part = x.astype(jnp.bfloat16)
            x = x - part.astype(jnp.float32)
            moved = jnp.dot(part, order, preferred_element_type=jnp.float32)
            total = moved if total is None else total + moved
        for zhi in range(2):
            at = 1536 * zhi + WIDE * q
            rows_ref[:, at : at + WIDE] = total[:, WIDE * zhi : WIDE * zhi + WIDE]
    for i in range(16):
        out_ref[i] = rows_ref[...]


def split_kernel(x_ref, high_ref, low_ref):
    x = x_ref[...]
    high = x.astype(jnp.bfloat16)
    high_ref[...] = high
    low_ref[...] = (x - high.astype(jnp.float32)).astype(jnp.bfloat16)


def product_kernel(high_ref, low_ref, panel_ref, out_ref, total_ref):
    step = pl.program_id(0)
    b = panel_ref[...]
    b_high = b.astype(jnp.bfloat16)
    b_low = (b - b_high.astype(jnp.float32)).astype(jnp.bfloat16)
    a_high, a_low = high_ref[...], low_ref[...]
    dot = functools.partial(jnp.dot, preferred_element_type=jnp.float32)
    term = dot(a_high, b_high) + (dot(a_low, b_high) + dot(a_high, b_low))

    @pl.when(step == 0)
    def _():
        total_ref[...] = term

    @pl.when(step > 0)
    def _():
        total_ref[...] += term

    @pl.when(step == HALF // STEP - 1)
    def _():
        for d in range(32):
            for g in range(3):
                out_ref[d, ROWS * g : ROWS * g + ROWS, :] = total_ref[
                    ROWS * d : ROWS * d + ROWS, 128 * g : 128 * g + 128
                ]


def divide_kernel(parts_ref, row_ref, col_ref, out_ref):
    row = row_ref[...]
    for i in range(16):
        for g in range(3):
            at = slice(ROWS * g, ROWS * g + ROWS)
            lanes = slice(WIDE * i + 128 * g, WIDE * i + 128 * g + 128)
            cycle = parts_ref[2 * i, at, :] + parts_ref[2 * i + 1, at, :]
            out_ref[:, lanes] = cycle / (row + col_ref[:, lanes])


def per_device(amplitudes, integrals, occupied_energy, virtual_energy, window_i, window_j):
    f32, bf16 = jnp.float32, jnp.bfloat16
    core = lax.axis_index("core").reshape(1)
    own, other, blocks = pl.pallas_call(
        prepare_kernel,
        out_shape=[
            jax.ShapeDtypeStruct((ROWS, HALF), f32),
            jax.ShapeDtypeStruct((ROWS, HALF), f32),
            jax.ShapeDtypeStruct((16, ROWS, WIDE), f32),
        ],
        in_specs=[pl.BlockSpec(memory_space=pltpu.SMEM), VMEM, VMEM],
        out_specs=[VMEM] * 3,
        compiler_params=params(),
        cost_estimate=cost(1, 2 << 20),
        name="prepare",
    )(core, amplitudes, integrals)
    other = lax.ppermute(other, "core", [(0, 1), (1, 0)])
    blocks = lax.all_to_all(blocks, PLANE, split_axis=0, concat_axis=0, tiled=True)
    panel = lax.all_gather(blocks.reshape(16 * ROWS, WIDE), RING, axis=0, tiled=True)

    spread = pl.pallas_call(
        spread_kernel,
        out_shape=jax.ShapeDtypeStruct((16, 2 * ROWS, HALF), f32),
        in_specs=[pl.BlockSpec(memory_space=pltpu.SMEM), VMEM, VMEM, VMEM],
        out_specs=VMEM,
        scratch_shapes=[pltpu.VMEM((2 * ROWS, HALF), f32)],
        compiler_params=params(),
        cost_estimate=cost(2 * 24 * 3 * HALF * 768, 7 << 20),
        name="spread",
    )(core, own, other, jnp.asarray(column_order()))
    spread, occupied_energy, virtual_energy, window_i, window_j = lax.optimization_barrier(
        (spread, occupied_energy, virtual_energy, window_i, window_j)
    )
    left = lax.all_to_all(spread, PLANE, split_axis=0, concat_axis=0, tiled=True)
    left = left.reshape(WIDE, HALF)
    tile = pl.BlockSpec((WIDE, STEP), lambda k: (0, k))
    high, low = pl.pallas_call(
        split_kernel,
        grid=(HALF // STEP,),
        out_shape=[jax.ShapeDtypeStruct((WIDE, HALF), bf16)] * 2,
        in_specs=[tile],
        out_specs=[tile, tile],
        compiler_params=params(),
        cost_estimate=cost(4 * WIDE * HALF, 8 * WIDE * HALF),
        name="split",
    )(left)

    index = lax.axis_index(AXES) * ROWS
    virt = virtual_energy.shape[0]
    row = occupied_energy[window_i[index // virt]] - lax.dynamic_slice_in_dim(
        virtual_energy, index % virt, ROWS, 0
    )
    col = (occupied_energy[window_j][:, None] - virtual_energy[None, :]).reshape(1, -1)
    row = row[:, None]
    high, low, row, col = lax.optimization_barrier((high, low, row, col))

    partial = pl.pallas_call(
        product_kernel,
        grid=(HALF // STEP,),
        out_shape=jax.ShapeDtypeStruct((32, 3 * ROWS, 128), f32),
        in_specs=[tile, tile, pl.BlockSpec((STEP, WIDE), lambda k: (k, 0))],
        out_specs=pl.BlockSpec((32, 3 * ROWS, 128), lambda k: (0, 0, 0)),
        scratch_shapes=[pltpu.VMEM((WIDE, WIDE), f32)],
        compiler_params=params(),
        cost_estimate=cost(6 * WIDE * WIDE * HALF, 8 * WIDE * HALF),
        name="product",
    )(high, low, panel)
    parts = lax.all_to_all(partial, ("y", "x", "core"), split_axis=0, concat_axis=0, tiled=True)
    return pl.pallas_call(
        divide_kernel,
        out_shape=jax.ShapeDtypeStruct((ROWS, 16 * WIDE), f32),
        in_specs=[VMEM] * 3,
        out_specs=VMEM,
        compiler_params=params(),
        cost_estimate=cost(4 * ROWS * 16 * WIDE, 1 << 20),
        name="divide",
    )(parts, row, col)


def solution(mesh):
    fine = Mesh(mesh.devices.reshape(SIZES), AXES)
    split = P(AXES, None)
    return jax.shard_map(
        per_device,
        mesh=fine,
        in_specs=(split, split, P(), P(), P(), P()),
        out_specs=split,
        check_vma=False,
    )
```

```python
import jax
import jax.numpy as jnp
import numpy as np
from jax import lax
from jax.experimental import pallas as pl
from jax.experimental.pallas import tpu as pltpu
from jax.sharding import Mesh, PartitionSpec as P

AXES = ("zlo", "core", "y", "x", "zhi")
SIZES = (8, 2, 4, 4, 2)
PLANE = ("y", "x")
RING = ("zhi", "zlo")
VIRT = 1536
OCC_WIN = 4
ROWS = 12
WIDE = 384
HALF = 3072
STEP = 512
VMEM = pl.BlockSpec(memory_space=pltpu.VMEM)


def params(mib):
    return pltpu.CompilerParams(vmem_limit_bytes=mib * 1024 * 1024)


def cost(flops, moved):
    return pl.CostEstimate(flops=flops, bytes_accessed=moved, transcendentals=0)


def column_source():
    return np.arange(768, dtype=np.int32).reshape(2, 16, 2, 12).transpose(2, 0, 1, 3).reshape(1, 768)


def blocks_kernel(b_ref, out_ref, sems):
    copies = [
        pltpu.make_async_copy(b_ref.at[:, WIDE * i : WIDE * i + WIDE], out_ref.at[i], sems.at[i])
        for i in range(16)
    ]
    for copy in copies:
        copy.start()
    for copy in copies:
        copy.wait()


def halves_kernel(core_ref, a_ref, own_ref, other_ref, sems):
    core = core_ref[0]
    copies = []
    for z in range(8):
        at = slice(WIDE * z, WIDE * z + WIDE)
        near = pl.ds(pl.multiple_of(768 * z + WIDE * core, 128), WIDE)
        far = pl.ds(pl.multiple_of(768 * z + WIDE - WIDE * core, 128), WIDE)
        copies.append(pltpu.make_async_copy(a_ref.at[:, far], other_ref.at[:, at], sems.at[z]))
        copies.append(pltpu.make_async_copy(a_ref.at[:, near], own_ref.at[:, at], sems.at[8 + z]))
    for copy in copies:
        copy.start()
    for copy in copies:
        copy.wait()


def spread_kernel(core_ref, own_ref, other_ref, source_ref, out_ref):
    first = core_ref[0] == 0
    own, other = own_ref[...], other_ref[...]
    upper, lower = jnp.where(first, own, other), jnp.where(first, other, own)
    x = jnp.concatenate([upper, lower], axis=0)
    parts = []
    for _ in range(3):
        part = x.astype(jnp.bfloat16)
        x = x - part.astype(jnp.float32)
        parts += [part[:, 768 * q : 768 * q + 768] for q in range(4)]
    parts = jnp.concatenate(parts, axis=0)
    wanted = lax.broadcasted_iota(jnp.int32, (768, 768), 0) == source_ref[...]
    order = jnp.where(wanted, 1.0, 0.0).astype(jnp.bfloat16)
    moved = jnp.dot(parts, order, preferred_element_type=jnp.float32)
    for q in range(4):
        rows = [moved[24 * (4 * p + q) : 24 * (4 * p + q) + 24] for p in range(3)]
        total = (rows[0] + rows[1]) + rows[2]
        for i in range(16):
            for zhi in range(2):
                at = 1536 * zhi + WIDE * q
                out_ref[i, :, at : at + WIDE] = total[:, WIDE * zhi : WIDE * zhi + WIDE]


def in_two(x):
    high = x.astype(jnp.bfloat16)
    return high, (x - high.astype(jnp.float32)).astype(jnp.bfloat16)


def split_kernel(x_ref, high_ref, low_ref):
    high_ref[...], low_ref[...] = in_two(x_ref[...])


def product_kernel(high_ref, low_ref, panel_ref, out_ref, highs, lows, panels, total_ref, sems):
    steps = HALF // STEP
    copies = []
    for k in range(steps):
        at = pl.ds(STEP * k, STEP)
        copies.append(
            [
                pltpu.make_async_copy(panel_ref.at[at], panels.at[k], sems.at[0, k]),
                pltpu.make_async_copy(high_ref.at[:, at], highs.at[k], sems.at[1, k]),
                pltpu.make_async_copy(low_ref.at[:, at], lows.at[k], sems.at[2, k]),
            ]
        )
        for copy in copies[k]:
            copy.start()
    for k in range(steps):
        for copy in copies[k]:
            copy.wait()
        a_high, a_low = highs[k], lows[k]
        b_high, b_low = in_two(panels[k])
        term = jnp.dot(
            jnp.concatenate([a_high, a_low, a_high], axis=1),
            jnp.concatenate([b_high, b_high, b_low], axis=0),
            preferred_element_type=jnp.float32,
        )
        if k == 0:
            total_ref[...] = term
        else:
            total_ref[...] += term
    for d in range(32):
        for g in range(3):
            out_ref[d, ROWS * g : ROWS * g + ROWS, :] = total_ref[
                ROWS * d : ROWS * d + ROWS, 128 * g : 128 * g + 128
            ]


def shifts_kernel(place_ref, wi_ref, wj_ref, occ_ref, virt_ref, lanes_ref, row_ref, col_ref):
    place = place_ref[0]
    per_orbital = VIRT // ROWS
    occ_i = occ_ref[wi_ref[place // per_orbital]]
    start = lax.rem(place, per_orbital) * ROWS
    at = lax.broadcasted_iota(jnp.int32, (ROWS, 128), 0)
    row = jnp.zeros((ROWS, 128), jnp.float32)
    for r in range(ROWS):
        row = jnp.where(at == r, occ_i - virt_ref[start + r], row)
    row_ref[...] = row
    for j in range(OCC_WIN):
        col_ref[:, VIRT * j : VIRT * j + VIRT] = occ_ref[wj_ref[j]] - lanes_ref[...]


def divide_kernel(parts_ref, row_ref, col_ref, out_ref):
    row = row_ref[...]
    for i in range(16):
        for g in range(3):
            at = slice(ROWS * g, ROWS * g + ROWS)
            lanes = slice(WIDE * i + 128 * g, WIDE * i + 128 * g + 128)
            cycle = parts_ref[2 * i, at, :] + parts_ref[2 * i + 1, at, :]
            out_ref[:, lanes] = cycle / (row + col_ref[:, lanes])


def per_device(amplitudes, integrals, occupied_energy, virtual_energy, window_i, window_j):
    f32 = jnp.float32
    place = lax.axis_index(AXES).reshape(1)
    core = lax.axis_index("core").reshape(1)
    place, core, integrals = lax.optimization_barrier((place, core, integrals))
    smem = pl.BlockSpec(memory_space=pltpu.SMEM)
    hbm = pl.BlockSpec(memory_space=pltpu.HBM)
    blocks = pl.pallas_call(
        blocks_kernel,
        out_shape=jax.ShapeDtypeStruct((16, ROWS, WIDE), f32),
        in_specs=[hbm],
        out_specs=VMEM,
        scratch_shapes=[pltpu.SemaphoreType.DMA((16,))],
        compiler_params=params(4),
        cost_estimate=cost(1, 1 << 20),
        name="blocks",
    )(integrals)
    blocks = lax.all_to_all(blocks, PLANE, split_axis=0, concat_axis=0, tiled=True)
    panel = lax.all_gather(blocks.reshape(16 * ROWS, WIDE), RING, axis=0, tiled=True)

    own, other = pl.pallas_call(
        halves_kernel,
        out_shape=[jax.ShapeDtypeStruct((ROWS, HALF), f32)] * 2,
        in_specs=[smem, hbm],
        out_specs=[VMEM] * 2,
        scratch_shapes=[pltpu.SemaphoreType.DMA((16,))],
        compiler_params=params(4),
        cost_estimate=cost(1, 1 << 20),
        name="halves",
    )(core, amplitudes)
    other = lax.ppermute(other, "core", [(0, 1), (1, 0)])
    spread = pl.pallas_call(
        spread_kernel,
        out_shape=jax.ShapeDtypeStruct((16, 2 * ROWS, HALF), f32),
        in_specs=[smem, VMEM, VMEM, VMEM],
        out_specs=VMEM,
        compiler_params=params(12),
        cost_estimate=cost(2 * 24 * 3 * HALF * 768, 7 << 20),
        name="spread",
    )(core, own, other, jnp.asarray(column_source()))
    left = lax.all_to_all(spread, PLANE, split_axis=0, concat_axis=0, tiled=True)
    left = left.reshape(WIDE, HALF)

    left, place, window_i, window_j, occupied_energy, virtual_energy = lax.optimization_barrier(
        (left, place, window_i, window_j, occupied_energy, virtual_energy)
    )
    row, col = pl.pallas_call(
        shifts_kernel,
        out_shape=[
            jax.ShapeDtypeStruct((ROWS, 128), f32),
            jax.ShapeDtypeStruct((1, OCC_WIN * VIRT), f32),
        ],
        in_specs=[smem] * 5 + [VMEM],
        out_specs=[VMEM] * 2,
        compiler_params=params(2),
        cost_estimate=cost(1, 1 << 16),
        name="shifts",
    )(place, window_i, window_j, occupied_energy, virtual_energy, virtual_energy[None, :])
    tile = pl.BlockSpec((WIDE, STEP), lambda k: (0, k))
    high, low = pl.pallas_call(
        split_kernel,
        grid=(HALF // STEP,),
        out_shape=[jax.ShapeDtypeStruct((WIDE, HALF), jnp.bfloat16)] * 2,
        in_specs=[tile],
        out_specs=[tile, tile],
        compiler_params=params(8),
        cost_estimate=cost(4 * WIDE * HALF, 8 * WIDE * HALF),
        name="split",
    )(left)
    high, low, row, col = lax.optimization_barrier((high, low, row, col))
    steps = HALF // STEP
    partial = pl.pallas_call(
        product_kernel,
        out_shape=jax.ShapeDtypeStruct((32, 3 * ROWS, 128), f32),
        in_specs=[hbm] * 3,
        out_specs=VMEM,
        scratch_shapes=[
            pltpu.VMEM((steps, WIDE, STEP), jnp.bfloat16),
            pltpu.VMEM((steps, WIDE, STEP), jnp.bfloat16),
            pltpu.VMEM((steps, STEP, WIDE), f32),
            pltpu.VMEM((WIDE, WIDE), f32),
            pltpu.SemaphoreType.DMA((3, steps)),
        ],
        compiler_params=params(56),
        cost_estimate=cost(6 * WIDE * WIDE * HALF, 8 * WIDE * HALF),
        name="product",
    )(high, low, panel)
    parts = lax.all_to_all(partial, ("y", "x", "core"), split_axis=0, concat_axis=0, tiled=True)
    return pl.pallas_call(
        divide_kernel,
        out_shape=jax.ShapeDtypeStruct((ROWS, 16 * WIDE), f32),
        in_specs=[VMEM] * 3,
        out_specs=VMEM,
        compiler_params=params(6),
        cost_estimate=cost(4 * ROWS * 16 * WIDE, 1 << 20),
        name="divide",
    )(parts, row, col)


def solution(mesh):
    fine = Mesh(mesh.devices.reshape(SIZES), AXES)
    split = P(AXES, None)
    return jax.shard_map(
        per_device,
        mesh=fine,
        in_specs=(split, split, P(), P(), P(), P()),
        out_specs=split,
        check_vma=False,
    )
```

```python
import jax
import jax.numpy as jnp
import numpy as np
from jax import lax
from jax.experimental import pallas as pl
from jax.experimental.pallas import tpu as pltpu
from jax.sharding import Mesh, PartitionSpec as P

AXES = ("zl4", "zb", "core", "y", "x", "zhi")
SIZES = (4, 2, 2, 4, 4, 2)
PLANE = ("y", "x")
VIRT = 1536
OCC_WIN = 4
ROWS = 12
WIDE = 384
SHARD = 16 * ROWS
DEEP = 8 * SHARD
STEP = 512
VMEM = pl.BlockSpec(memory_space=pltpu.VMEM)
SMEM = pl.BlockSpec(memory_space=pltpu.SMEM)
HBM = pl.BlockSpec(memory_space=pltpu.HBM)
F32 = jnp.float32
BF16 = jnp.bfloat16


def call(body, name, out, ins, outs, mib, flops, moved, scratch=(), grid=None):
    return pl.pallas_call(
        body,
        out_shape=out,
        in_specs=ins,
        out_specs=outs,
        scratch_shapes=scratch,
        compiler_params=pltpu.CompilerParams(vmem_limit_bytes=mib * 1024 * 1024),
        cost_estimate=pl.CostEstimate(flops=flops, bytes_accessed=moved, transcendentals=0),
        name=name,
    )


def shape(*dims, dtype=F32):
    return jax.ShapeDtypeStruct(dims, dtype)


def column_source():
    return np.arange(WIDE, dtype=np.int32).reshape(16, 2, ROWS).transpose(1, 0, 2).reshape(1, WIDE)


def in_two(x):
    high = x.astype(BF16)
    return high, (x - high.astype(F32)).astype(BF16)


def first_kernel(where_ref, a_ref, b_ref, own_ref, other_ref, blocks_ref):
    zb = where_ref[0]
    for z in range(4):
        at = slice(768 * z, 768 * z + 768)
        other_ref[:, at] = a_ref[:, pl.ds(pl.multiple_of(1536 * z + 768 - 768 * zb, 128), 768)]
        own_ref[:, at] = a_ref[:, pl.ds(pl.multiple_of(1536 * z + 768 * zb, 128), 768)]
    for i in range(16):
        blocks_ref[i] = b_ref[:, WIDE * i : WIDE * i + WIDE]


def spread_kernel(where_ref, own_ref, other_ref, source_ref, out_ref):
    first = where_ref[0] == 0
    own, other = own_ref[...], other_ref[...]
    upper, lower = jnp.where(first, own, other), jnp.where(first, other, own)
    x = jnp.concatenate([upper, lower], axis=0)
    parts = []
    for _ in range(3):
        part = x.astype(BF16)
        x = x - part.astype(F32)
        parts += [part[:, WIDE * q : WIDE * q + WIDE] for q in range(8)]
    parts = jnp.concatenate(parts, axis=0)
    wanted = lax.broadcasted_iota(jnp.int32, (WIDE, WIDE), 0) == source_ref[...]
    order = jnp.where(wanted, 1.0, 0.0).astype(BF16)
    moved = jnp.dot(parts, order, preferred_element_type=F32)
    for q in range(8):
        rows = [moved[24 * (8 * p + q) : 24 * (8 * p + q) + 24] for p in range(3)]
        total = (rows[0] + rows[1]) + rows[2]
        z, core = divmod(q, 2)
        for i in range(16):
            out_ref[16 * core + i, :, WIDE * z : WIDE * z + WIDE] = total


def place_kernel(where_ref, *refs):
    shards, high_ref, low_ref = refs[:-2], refs[-2], refs[-1]
    ring = where_ref[2]
    steps = [0, -1, 1, -2, 2, -3, 3, 4, 4]
    for i, step in enumerate(steps):
        at = lax.rem(ring + 8 + step, 8)
        row = (lax.rem(at, 4) * 2 + at // 4) * SHARD + (SHARD // 2 if i == 8 else 0)
        rows = pl.ds(pl.multiple_of(row, 32), shards[i].shape[0])
        high_ref[rows, :], low_ref[rows, :] = in_two(shards[i][...])


def product_kernel(mine, where_ref, left_ref, high_ref, low_ref, out_ref, chunks_ref, sems):
    half = where_ref[1] if mine else 1 - where_ref[1]
    copies = []
    for k in range(DEEP // STEP):
        source = left_ref.at[half, :, pl.ds(STEP * k, STEP)]
        copies.append(pltpu.make_async_copy(source, chunks_ref.at[k], sems.at[k]))
        copies[k].start()
    total = None
    for k, copy in enumerate(copies):
        copy.wait()
        a_high, a_low = in_two(chunks_ref[k])
        at = slice(STEP * k, STEP * k + STEP)
        b_high, b_low = high_ref[at, :], low_ref[at, :]
        term = jnp.dot(
            jnp.concatenate([a_high, a_low, a_high], axis=1),
            jnp.concatenate([b_high, b_high, b_low], axis=0),
            preferred_element_type=F32,
        )
        total = term if total is None else total + term
    out_ref[...] = total


def pack_kernel(own_ref, other_ref, out_ref):
    for i in range(16):
        for zb in range(2):
            rows = slice(24 * i + ROWS * zb, 24 * i + ROWS * zb + ROWS)
            total = own_ref[rows, :] + other_ref[rows, :]
            for g in range(3):
                at = slice(ROWS * g, ROWS * g + ROWS)
                out_ref[16 * zb + i, at, :] = total[:, 128 * g : 128 * g + 128]


def shifts_kernel(where_ref, wi_ref, wj_ref, occ_ref, virt_ref, lanes_ref, row_ref, col_ref):
    place = where_ref[3]
    per_orbital = VIRT // ROWS
    occ_i = occ_ref[wi_ref[place // per_orbital]]
    start = lax.rem(place, per_orbital) * ROWS
    at = lax.broadcasted_iota(jnp.int32, (ROWS, 128), 0)
    row = jnp.zeros((ROWS, 128), F32)
    for r in range(ROWS):
        row = jnp.where(at == r, occ_i - virt_ref[start + r], row)
    row_ref[...] = row
    for j in range(OCC_WIN):
        col_ref[:, VIRT * j : VIRT * j + VIRT] = occ_ref[wj_ref[j]] - lanes_ref[...]


def divide_kernel(parts_ref, row_ref, col_ref, out_ref):
    row = row_ref[...]
    for i in range(16):
        for g in range(3):
            at = slice(ROWS * g, ROWS * g + ROWS)
            lanes = slice(WIDE * i + 128 * g, WIDE * i + 128 * g + 128)
            cycle = parts_ref[i, at, :] + parts_ref[16 + i, at, :]
            out_ref[:, lanes] = cycle / (row + col_ref[:, lanes])


def turn(x, step):
    index = lambda a: (a % 8 % 4) * 2 + a % 8 // 4
    return lax.ppermute(x, ("zl4", "zhi"), [(index(a), index(a + step)) for a in range(8)])


def per_device(amplitudes, integrals, occupied_energy, virtual_energy, window_i, window_j):
    swap = [(0, 1), (1, 0)]
    axis = lax.axis_index
    where = jnp.stack([axis("zb"), axis("core"), axis("zhi") * 4 + axis("zl4"), axis(AXES)])
    own, other, blocks = call(
        first_kernel,
        "first",
        [shape(ROWS, 3072), shape(ROWS, 3072), shape(16, ROWS, WIDE)],
        [SMEM, VMEM, VMEM],
        [VMEM] * 3,
        4,
        1,
        2 << 20,
    )(where, amplitudes, integrals)
    other = lax.ppermute(other, "zb", swap)
    blocks = lax.all_to_all(blocks, PLANE, split_axis=0, concat_axis=0, tiled=True)
    shard = blocks.reshape(SHARD, WIDE)

    shards, right, left = [shard], shard, shard
    for _ in range(3):
        right, left = turn(right, 1), turn(left, -1)
        shards += [right, left]
    shards += [turn(right[: SHARD // 2], 1), turn(left[SHARD // 2 :], -1)]

    spread = call(
        spread_kernel,
        "spread",
        shape(32, 2 * ROWS, DEEP),
        [SMEM, VMEM, VMEM, VMEM],
        VMEM,
        14,
        2 * 576 * WIDE * WIDE,
        6 << 20,
    )(where, own, other, jnp.asarray(column_source()))
    rows = lax.all_to_all(spread, ("core", "y", "x"), split_axis=0, concat_axis=0, tiled=True)
    rows = rows.reshape(2, WIDE, DEEP)

    row, col = call(
        shifts_kernel,
        "shifts",
        [shape(ROWS, 128), shape(1, OCC_WIN * VIRT)],
        [SMEM] * 5 + [VMEM],
        [VMEM] * 2,
        2,
        1,
        1 << 16,
    )(where, window_i, window_j, occupied_energy, virtual_energy, virtual_energy[None, :])
    high, low = call(
        place_kernel,
        "place",
        [shape(DEEP, WIDE, dtype=BF16)] * 2,
        [SMEM] + [VMEM] * 9,
        [VMEM] * 2,
        10,
        4 * DEEP * WIDE,
        8 * DEEP * WIDE,
    )(where, *shards)
    high, low, row, col = lax.optimization_barrier((high, low, row, col))

    def product(mine):
        return call(
            lambda *refs: product_kernel(mine, *refs),
            "product_own" if mine else "product_other",
            shape(WIDE, WIDE),
            [SMEM, HBM, VMEM, VMEM],
            VMEM,
            16,
            6 * WIDE * WIDE * DEEP,
            8 * WIDE * DEEP,
            [pltpu.VMEM((DEEP // STEP, WIDE, STEP), F32), pltpu.SemaphoreType.DMA((DEEP // STEP,))],
        )(where, rows, high, low)

    theirs = lax.ppermute(product(False), "core", swap)
    packed = call(
        pack_kernel,
        "pack",
        shape(32, 3 * ROWS, 128),
        [VMEM] * 2,
        VMEM,
        6,
        WIDE * WIDE,
        12 * WIDE * WIDE,
    )(product(True), theirs)
    parts = lax.all_to_all(packed, ("zb", "y", "x"), split_axis=0, concat_axis=0, tiled=True)
    return call(
        divide_kernel,
        "divide",
        shape(ROWS, 16 * WIDE),
        [VMEM] * 3,
        VMEM,
        6,
        4 * ROWS * 16 * WIDE,
        1 << 20,
    )(parts, row, col)


def solution(mesh):
    fine = Mesh(mesh.devices.reshape(SIZES), AXES)
    split = P(AXES, None)
    return jax.shard_map(
        per_device,
        mesh=fine,
        in_specs=(split, split, P(), P(), P(), P()),
        out_specs=split,
        check_vma=False,
    )
```

```python
import jax
import jax.numpy as jnp
import numpy as np
from jax import lax
from jax.experimental import pallas as pl
from jax.experimental.pallas import tpu as pltpu
from jax.sharding import Mesh, PartitionSpec as P

AXES = ("zl4", "zb", "core", "y", "x", "zhi")
SIZES = (4, 2, 2, 4, 4, 2)
PLANE = ("y", "x")
VIRT = 1536
OCC_WIN = 4
ROWS = 12
WIDE = 384
SHARD = 16 * ROWS
DEEP = 8 * SHARD
STEP = 512
TALL = 62
SPREAD = 52
VMEM = pl.BlockSpec(memory_space=pltpu.VMEM)
SMEM = pl.BlockSpec(memory_space=pltpu.SMEM)
HBM = pl.BlockSpec(memory_space=pltpu.HBM)
F32 = jnp.float32
BF16 = jnp.bfloat16


def call(body, name, out, ins, outs, mib, flops, moved, scratch=()):
    return pl.pallas_call(
        body,
        out_shape=out,
        in_specs=ins,
        out_specs=outs,
        scratch_shapes=scratch,
        compiler_params=pltpu.CompilerParams(vmem_limit_bytes=mib * 1024 * 1024),
        cost_estimate=pl.CostEstimate(flops=flops, bytes_accessed=moved, transcendentals=0),
        name=name,
    )


def shape(*dims, dtype=F32):
    return jax.ShapeDtypeStruct(dims, dtype)


def column_source():
    return np.arange(WIDE, dtype=np.int32).reshape(16, 2, ROWS).transpose(1, 0, 2).reshape(1, WIDE)


def in_two(x):
    high = x.astype(BF16)
    return high, (x - high.astype(F32)).astype(BF16)


def run(copies):
    for copy in copies:
        copy.start()
    for copy in copies:
        copy.wait()


def halves_kernel(where_ref, a_ref, own_ref, other_ref, sems):
    zb = where_ref[0]
    copies = []
    for z in range(4):
        at = slice(768 * z, 768 * z + 768)
        far = pl.ds(pl.multiple_of(1536 * z + 768 - 768 * zb, 128), 768)
        near = pl.ds(pl.multiple_of(1536 * z + 768 * zb, 128), 768)
        copies.append(pltpu.make_async_copy(a_ref.at[:, far], other_ref.at[:, at], sems.at[z]))
        copies.append(pltpu.make_async_copy(a_ref.at[:, near], own_ref.at[:, at], sems.at[4 + z]))
    run(copies)


def blocks_kernel(b_ref, out_ref, sems):
    run(
        [
            pltpu.make_async_copy(
                b_ref.at[:, WIDE * i : WIDE * i + WIDE], out_ref.at[i], sems.at[i]
            )
            for i in range(16)
        ]
    )


def stack_kernel(blocks_ref, out_ref):
    for i in range(16):
        out_ref[ROWS * i : ROWS * i + ROWS, :] = blocks_ref[i]


def half_kernel(lower, x_ref, out_ref):
    out_ref[...] = x_ref[SHARD // 2 :, :] if lower else x_ref[: SHARD // 2, :]


def spread_kernel(own_ref, pair_ref, source_ref, out_ref, rows_ref, sems):
    x = jnp.concatenate([own_ref[...], pair_ref[...]], axis=0)
    parts = []
    for _ in range(3):
        part = x.astype(BF16)
        x = x - part.astype(F32)
        parts += [part[:, WIDE * q : WIDE * q + WIDE] for q in range(8)]
    parts = jnp.concatenate(parts, axis=0)
    wanted = lax.broadcasted_iota(jnp.int32, (WIDE, WIDE), 0) == source_ref[...]
    order = jnp.where(wanted, 1.0, 0.0).astype(BF16)
    moved = jnp.dot(parts, order, preferred_element_type=F32)
    for q in range(8):
        rows = [moved[24 * (8 * p + q) : 24 * (8 * p + q) + 24] for p in range(3)]
        z, core = divmod(q, 2)
        rows_ref[core, :, WIDE * z : WIDE * z + WIDE] = (rows[0] + rows[1]) + rows[2]
    run([pltpu.make_async_copy(rows_ref.at[i // 16], out_ref.at[i], sems.at[i]) for i in range(32)])


def block_of(ring, step):
    at = lax.rem(ring + 8 + step, 8)
    return lax.rem(at, 4), at // 4


def place_kernel(where_ref, *refs):
    shards, high_ref, low_ref = refs[:7], refs[7], refs[8]
    ring = where_ref[2]
    for shard, step in zip(shards, [0, -1, 1, -2, 2, -3, 3]):
        z, zhi = block_of(ring, step)
        at = pl.ds(pl.multiple_of((2 * z + zhi) * SHARD, 64), SHARD)
        high_ref[at, :], low_ref[at, :] = in_two(shard[...])
    z, zhi = block_of(ring, 4)
    at = pl.ds(pl.multiple_of((2 * z + zhi) * SHARD, 64), SHARD)
    high_ref[at, :] = jnp.zeros((SHARD, WIDE), BF16)
    low_ref[at, :] = jnp.zeros((SHARD, WIDE), BF16)


def seven_kernel(where_ref, rows_ref, high_ref, low_ref, part_ref, run_high_ref, run_low_ref, left_ref, sems):
    copies = []
    for k in range(DEEP // STEP):
        at = pl.ds(STEP * k, STEP)
        for core in range(2):
            first = 16 * (1 - where_ref[1] if core else where_ref[1])
            source = rows_ref.at[pl.ds(first, 16), :, at]
            copies.append(pltpu.make_async_copy(source, left_ref.at[core, :, :, at], sems.at[core, k]))
            copies[-1].start()
    for k in range(DEEP // STEP):
        copies[2 * k].wait()
        copies[2 * k + 1].wait()
        at = slice(STEP * k, STEP * k + STEP)
        a_high, a_low = in_two(left_ref[:, :, :, at].reshape(2 * WIDE, STEP))
        b_high, b_low = high_ref[at, :], low_ref[at, :]
        term = jnp.dot(
            jnp.concatenate([a_high, a_low, a_high], axis=1),
            jnp.concatenate([b_high, b_high, b_low], axis=0),
            preferred_element_type=F32,
        )
        if k == 0:
            part_ref[...] = term
        else:
            part_ref[...] += term
    z, _ = block_of(where_ref[2], 4)
    last = left_ref[:, :, :, pl.ds(pl.multiple_of(z * WIDE, 128), WIDE)]
    run_high_ref[...], run_low_ref[...] = in_two(last.reshape(2 * WIDE, WIDE))


def eighth_kernel(where_ref, part_ref, a_high_ref, a_low_ref, up_ref, down_ref, own_ref, other_ref, high_ref, low_ref):
    _, zhi = block_of(where_ref[2], 4)
    high_ref[...] = jnp.zeros((WIDE, WIDE), BF16)
    low_ref[...] = jnp.zeros((WIDE, WIDE), BF16)
    for i, half in enumerate([up_ref, down_ref]):
        at = pl.ds(pl.multiple_of(zhi * SHARD + SHARD // 2 * i, 32), SHARD // 2)
        high_ref[at, :], low_ref[at, :] = in_two(half[...])
    a_high, a_low, b_high, b_low = a_high_ref[...], a_low_ref[...], high_ref[...], low_ref[...]
    total = part_ref[...] + jnp.dot(
        jnp.concatenate([a_high, a_low, a_high], axis=1),
        jnp.concatenate([b_high, b_high, b_low], axis=0),
        preferred_element_type=F32,
    )
    own_ref[...] = total[:WIDE]
    other_ref[...] = total[WIDE:]


def pack_kernel(where_ref, own_ref, other_ref, out_ref):
    for pair in range(2):
        zb = 1 - where_ref[0] if pair else where_ref[0]
        for i in range(16):
            rows = slice(24 * i + ROWS * pair, 24 * i + ROWS * pair + ROWS)
            total = own_ref[rows, :] + other_ref[rows, :]
            for g in range(3):
                at = slice(ROWS * g, ROWS * g + ROWS)
                out_ref[16 * zb + i, at, :] = total[:, 128 * g : 128 * g + 128]


def shifts_kernel(where_ref, wi_ref, wj_ref, occ_ref, virt_ref, lanes_ref, row_ref, col_ref):
    place = where_ref[3]
    per_orbital = VIRT // ROWS
    occ_i = occ_ref[wi_ref[place // per_orbital]]
    start = lax.rem(place, per_orbital) * ROWS
    at = lax.broadcasted_iota(jnp.int32, (ROWS, 128), 0)
    row = jnp.zeros((ROWS, 128), F32)
    for r in range(ROWS):
        row = jnp.where(at == r, occ_i - virt_ref[start + r], row)
    row_ref[...] = row
    for j in range(OCC_WIN):
        col_ref[:, VIRT * j : VIRT * j + VIRT] = occ_ref[wj_ref[j]] - lanes_ref[...].reshape(1, VIRT)


def divide_kernel(parts_ref, row_ref, col_ref, out_ref):
    row = row_ref[...]
    for i in range(16):
        for g in range(3):
            at = slice(ROWS * g, ROWS * g + ROWS)
            lanes = slice(WIDE * i + 128 * g, WIDE * i + 128 * g + 128)
            cycle = parts_ref[i, at, :] + parts_ref[16 + i, at, :]
            out_ref[:, lanes] = cycle / (row + col_ref[:, lanes])


def turn(x, step):
    index = lambda a: (a % 8 % 4) * 2 + a % 8 // 4
    return lax.ppermute(x, ("zl4", "zhi"), [(index(a), index(a + step)) for a in range(8)])


def per_device(amplitudes, integrals, occupied_energy, virtual_energy, window_i, window_j):
    swap = [(0, 1), (1, 0)]
    axis = lax.axis_index
    where = jnp.stack([axis("zb"), axis("core"), axis("zhi") * 4 + axis("zl4"), axis(AXES)])
    own, pair = call(
        halves_kernel,
        "halves",
        [shape(ROWS, 3072)] * 2,
        [SMEM, HBM],
        [VMEM] * 2,
        4,
        1,
        1 << 20,
        [pltpu.SemaphoreType.DMA((8,))],
    )(where, amplitudes)
    pair = lax.ppermute(pair, "zb", swap)
    blocks = call(
        blocks_kernel,
        "blocks",
        shape(16, ROWS, WIDE),
        [HBM],
        VMEM,
        TALL,
        1,
        1 << 20,
        [pltpu.SemaphoreType.DMA((16,))],
    )(integrals)
    blocks = lax.all_to_all(blocks, PLANE, split_axis=0, concat_axis=0, tiled=True)
    shard = call(
        stack_kernel,
        "stack",
        shape(SHARD, WIDE),
        [VMEM],
        VMEM,
        4,
        1,
        1 << 20,
    )(blocks)

    shards, right, left = [shard], shard, shard
    for _ in range(3):
        right, left = turn(right, 1), turn(left, -1)
        shards += [right, left]
    def half(x, lower):
        return call(
            lambda *refs: half_kernel(lower, *refs),
            "lower_half" if lower else "upper_half",
            shape(SHARD // 2, WIDE),
            [VMEM],
            VMEM,
            2,
            1,
            1 << 19,
        )(x)

    up, down = turn(half(right, False), 1), turn(half(left, True), -1)


    spread = call(
        spread_kernel,
        "spread",
        shape(32, 2 * ROWS, DEEP),
        [VMEM] * 3,
        HBM,
        SPREAD,
        2 * 576 * WIDE * WIDE,
        6 << 20,
        [pltpu.VMEM((2, 2 * ROWS, DEEP), F32), pltpu.SemaphoreType.DMA((32,))],
    )(own, pair, jnp.asarray(column_source()))
    rows = lax.all_to_all(spread, ("core", "y", "x"), split_axis=0, concat_axis=0, tiled=True)

    row, col = call(
        shifts_kernel,
        "shifts",
        [shape(ROWS, 128), shape(1, OCC_WIN * VIRT)],
        [SMEM] * 5 + [VMEM],
        [VMEM] * 2,
        2,
        1,
        1 << 16,
    )(where, window_i, window_j, occupied_energy, virtual_energy, virtual_energy)
    high, low = call(
        place_kernel,
        "place",
        [shape(DEEP, WIDE, dtype=BF16)] * 2,
        [SMEM] + [VMEM] * 7,
        [VMEM] * 2,
        10,
        4 * DEEP * WIDE,
        8 * DEEP * WIDE,
    )(where, *shards)
    part, run_high, run_low = call(
        seven_kernel,
        "seven",
        [shape(2 * WIDE, WIDE)] + [shape(2 * WIDE, WIDE, dtype=BF16)] * 2,
        [SMEM, HBM] + [VMEM] * 2,
        [VMEM] * 3,
        24,
        12 * WIDE * WIDE * DEEP,
        12 * WIDE * DEEP,
        [pltpu.VMEM((2, 16, 2 * ROWS, DEEP), F32), pltpu.SemaphoreType.DMA((2, DEEP // STEP))],
    )(where, rows, high, low)
    part, run_high, run_low, row, col = lax.optimization_barrier(
        (part, run_high, run_low, row, col)
    )
    mine, theirs = call(
        eighth_kernel,
        "eighth",
        [shape(WIDE, WIDE)] * 2,
        [SMEM] + [VMEM] * 5,
        [VMEM] * 2,
        14,
        12 * WIDE * WIDE * WIDE,
        6 << 20,
        [pltpu.VMEM((WIDE, WIDE), BF16)] * 2,
    )(where, part, run_high, run_low, up, down)
    theirs = lax.ppermute(theirs, "core", swap)
    packed = call(
        pack_kernel,
        "pack",
        shape(32, 3 * ROWS, 128),
        [SMEM] + [VMEM] * 2,
        VMEM,
        6,
        WIDE * WIDE,
        12 * WIDE * WIDE,
    )(where, mine, theirs)
    parts = lax.all_to_all(packed, ("zb", "y", "x"), split_axis=0, concat_axis=0, tiled=True)
    return call(
        divide_kernel,
        "divide",
        shape(ROWS, 16 * WIDE),
        [VMEM] * 3,
        VMEM,
        6,
        4 * ROWS * 16 * WIDE,
        1 << 20,
    )(parts, row, col)


def solution(mesh):
    fine = Mesh(mesh.devices.reshape(SIZES), AXES)
    split = P(AXES, None)
    return jax.shard_map(
        per_device,
        mesh=fine,
        in_specs=(split, split, P(), P(), P(), P()),
        out_specs=split,
        check_vma=False,
    )
```

```python
import jax
import jax.numpy as jnp
import numpy as np
from jax import lax
from jax.experimental import pallas as pl
from jax.experimental.pallas import tpu as pltpu
from jax.sharding import Mesh, PartitionSpec as P

AXES = ("zl4", "zb", "core", "y", "x", "zhi")
SIZES = (4, 2, 2, 4, 4, 2)
PLANE = ("y", "x")
VIRT = 1536
OCC_WIN = 4
ROWS = 12
WIDE = 384
SHARD = 16 * ROWS
DEEP = 8 * SHARD
STEP = 512
TALL = 62
SPREAD = 52
VMEM = pl.BlockSpec(memory_space=pltpu.VMEM)
SMEM = pl.BlockSpec(memory_space=pltpu.SMEM)
HBM = pl.BlockSpec(memory_space=pltpu.HBM)
F32 = jnp.float32
BF16 = jnp.bfloat16


def call(body, name, out, ins, outs, mib, flops, moved, scratch=()):
    return pl.pallas_call(
        body,
        out_shape=out,
        in_specs=ins,
        out_specs=outs,
        scratch_shapes=scratch,
        compiler_params=pltpu.CompilerParams(vmem_limit_bytes=mib * 1024 * 1024),
        cost_estimate=pl.CostEstimate(flops=flops, bytes_accessed=moved, transcendentals=0),
        name=name,
    )


def shape(*dims, dtype=F32):
    return jax.ShapeDtypeStruct(dims, dtype)


def column_source():
    return np.arange(WIDE, dtype=np.int32).reshape(16, 2, ROWS).transpose(1, 0, 2).reshape(1, WIDE)


def in_two(x):
    high = x.astype(BF16)
    return high, (x - high.astype(F32)).astype(BF16)


def run(copies):
    for copy in copies:
        copy.start()
    for copy in copies:
        copy.wait()


def halves_kernel(where_ref, a_ref, own_ref, other_ref, sems):
    zb = where_ref[0]
    copies = []
    for z in range(4):
        at = slice(768 * z, 768 * z + 768)
        far = pl.ds(pl.multiple_of(1536 * z + 768 - 768 * zb, 128), 768)
        near = pl.ds(pl.multiple_of(1536 * z + 768 * zb, 128), 768)
        copies.append(pltpu.make_async_copy(a_ref.at[:, far], other_ref.at[:, at], sems.at[z]))
        copies.append(pltpu.make_async_copy(a_ref.at[:, near], own_ref.at[:, at], sems.at[4 + z]))
    run(copies)


def blocks_kernel(b_ref, out_ref, sems):
    run(
        [
            pltpu.make_async_copy(
                b_ref.at[:, WIDE * i : WIDE * i + WIDE], out_ref.at[i], sems.at[i]
            )
            for i in range(16)
        ]
    )


def stack_kernel(blocks_ref, out_ref):
    for i in range(16):
        out_ref[ROWS * i : ROWS * i + ROWS, :] = blocks_ref[i]


def half_kernel(lower, x_ref, out_ref):
    out_ref[...] = x_ref[SHARD // 2 :, :] if lower else x_ref[: SHARD // 2, :]


def spread_kernel(own_ref, pair_ref, source_ref, out_ref, rows_ref, sems):
    x = jnp.concatenate([own_ref[...], pair_ref[...]], axis=0)
    parts = []
    for _ in range(3):
        part = x.astype(BF16)
        x = x - part.astype(F32)
        parts += [part[:, WIDE * q : WIDE * q + WIDE] for q in range(8)]
    parts = jnp.concatenate(parts, axis=0)
    wanted = lax.broadcasted_iota(jnp.int32, (WIDE, WIDE), 0) == source_ref[...]
    order = jnp.where(wanted, 1.0, 0.0).astype(BF16)
    moved = jnp.dot(parts, order, preferred_element_type=F32)
    for q in range(8):
        rows = [moved[24 * (8 * p + q) : 24 * (8 * p + q) + 24] for p in range(3)]
        z, core = divmod(q, 2)
        rows_ref[core, :, WIDE * z : WIDE * z + WIDE] = (rows[0] + rows[1]) + rows[2]
    run([pltpu.make_async_copy(rows_ref.at[i % 2], out_ref.at[i], sems.at[i]) for i in range(32)])


def block_of(ring, step):
    at = lax.rem(ring + 8 + step, 8)
    return lax.rem(at, 4), at // 4


def place_kernel(where_ref, *refs):
    shards, high_ref, low_ref = refs[:7], refs[7], refs[8]
    ring = where_ref[2]
    for shard, step in zip(shards, [0, -1, 1, -2, 2, -3, 3]):
        z, zhi = block_of(ring, step)
        at = pl.ds(pl.multiple_of((2 * z + zhi) * SHARD, 64), SHARD)
        high_ref[at, :], low_ref[at, :] = in_two(shard[...])
    z, zhi = block_of(ring, 4)
    at = pl.ds(pl.multiple_of((2 * z + zhi) * SHARD, 64), SHARD)
    high_ref[at, :] = jnp.zeros((SHARD, WIDE), BF16)
    low_ref[at, :] = jnp.zeros((SHARD, WIDE), BF16)


def seven_kernel(where_ref, rows_ref, high_ref, low_ref, part_ref, run_high_ref, run_low_ref, left_ref, sems):
    copies = []
    for k in range(DEEP // STEP):
        at = pl.ds(STEP * k, STEP)
        for core in range(2):
            which = 1 - where_ref[1] if core else where_ref[1]
            source = rows_ref.at[:, which, :, at]
            copies.append(pltpu.make_async_copy(source, left_ref.at[core, :, :, at], sems.at[core, k]))
            copies[-1].start()
    for k in range(DEEP // STEP):
        copies[2 * k].wait()
        copies[2 * k + 1].wait()
        at = slice(STEP * k, STEP * k + STEP)
        a_high, a_low = in_two(left_ref[:, :, :, at].reshape(2 * WIDE, STEP))
        b_high, b_low = high_ref[at, :], low_ref[at, :]
        term = jnp.dot(
            jnp.concatenate([a_high, a_low, a_high], axis=1),
            jnp.concatenate([b_high, b_high, b_low], axis=0),
            preferred_element_type=F32,
        )
        if k == 0:
            part_ref[...] = term
        else:
            part_ref[...] += term
    z, _ = block_of(where_ref[2], 4)
    last = left_ref[:, :, :, pl.ds(pl.multiple_of(z * WIDE, 128), WIDE)]
    run_high_ref[...], run_low_ref[...] = in_two(last.reshape(2 * WIDE, WIDE))


def eighth_kernel(mine, where_ref, part_ref, a_high_ref, a_low_ref, last_ref, out_ref, high_ref, low_ref):
    _, zhi = block_of(where_ref[2], 4)
    high_ref[...] = jnp.zeros((WIDE, WIDE), BF16)
    low_ref[...] = jnp.zeros((WIDE, WIDE), BF16)
    at = pl.ds(pl.multiple_of(zhi * SHARD, 64), SHARD)
    high_ref[at, :], low_ref[at, :] = in_two(last_ref[...])
    rows = slice(0, WIDE) if mine else slice(WIDE, 2 * WIDE)
    a_high, a_low, b_high, b_low = a_high_ref[rows, :], a_low_ref[rows, :], high_ref[...], low_ref[...]
    out_ref[...] = part_ref[rows, :] + jnp.dot(
        jnp.concatenate([a_high, a_low, a_high], axis=1),
        jnp.concatenate([b_high, b_high, b_low], axis=0),
        preferred_element_type=F32,
    )


def pack_kernel(where_ref, own_ref, other_ref, out_ref):
    for pair in range(2):
        zb = 1 - where_ref[0] if pair else where_ref[0]
        for i in range(16):
            rows = slice(24 * i + ROWS * pair, 24 * i + ROWS * pair + ROWS)
            total = own_ref[rows, :] + other_ref[rows, :]
            for g in range(3):
                at = slice(ROWS * g, ROWS * g + ROWS)
                out_ref[16 * zb + i, at, :] = total[:, 128 * g : 128 * g + 128]


def shifts_kernel(where_ref, wi_ref, wj_ref, occ_ref, virt_ref, lanes_ref, row_ref, col_ref):
    place = where_ref[3]
    per_orbital = VIRT // ROWS
    occ_i = occ_ref[wi_ref[place // per_orbital]]
    start = lax.rem(place, per_orbital) * ROWS
    at = lax.broadcasted_iota(jnp.int32, (ROWS, 128), 0)
    row = jnp.zeros((ROWS, 128), F32)
    for r in range(ROWS):
        row = jnp.where(at == r, occ_i - virt_ref[start + r], row)
    row_ref[...] = row
    for j in range(OCC_WIN):
        col_ref[:, VIRT * j : VIRT * j + VIRT] = occ_ref[wj_ref[j]] - lanes_ref[...].reshape(1, VIRT)


def divide_kernel(parts_ref, row_ref, col_ref, out_ref):
    row = row_ref[...]
    for i in range(16):
        for g in range(3):
            at = slice(ROWS * g, ROWS * g + ROWS)
            lanes = slice(WIDE * i + 128 * g, WIDE * i + 128 * g + 128)
            cycle = parts_ref[i, at, :] + parts_ref[16 + i, at, :]
            out_ref[:, lanes] = cycle / (row + col_ref[:, lanes])


def turn(x, step):
    index = lambda a: (a % 8 % 4) * 2 + a % 8 // 4
    return lax.ppermute(x, ("zl4", "zhi"), [(index(a), index(a + step)) for a in range(8)])


def per_device(amplitudes, integrals, occupied_energy, virtual_energy, window_i, window_j):
    swap = [(0, 1), (1, 0)]
    axis = lax.axis_index
    where = jnp.stack([axis("zb"), axis("core"), axis("zhi") * 4 + axis("zl4"), axis(AXES)])
    own, pair = call(
        halves_kernel,
        "halves",
        [shape(ROWS, 3072)] * 2,
        [SMEM, HBM],
        [VMEM] * 2,
        4,
        1,
        1 << 20,
        [pltpu.SemaphoreType.DMA((8,))],
    )(where, amplitudes)
    pair = lax.ppermute(pair, "zb", swap)
    blocks = call(
        blocks_kernel,
        "blocks",
        shape(16, ROWS, WIDE),
        [HBM],
        VMEM,
        TALL,
        1,
        1 << 20,
        [pltpu.SemaphoreType.DMA((16,))],
    )(integrals)
    blocks = lax.all_to_all(blocks, PLANE, split_axis=0, concat_axis=0, tiled=True)
    shard = call(
        stack_kernel,
        "stack",
        shape(SHARD, WIDE),
        [VMEM],
        VMEM,
        4,
        1,
        1 << 20,
    )(blocks)

    shards, right, left = [shard], shard, shard
    for _ in range(3):
        right, left = turn(right, 1), turn(left, -1)
        shards += [right, left]
    last = turn(right, 1)


    spread = call(
        spread_kernel,
        "spread",
        shape(32, 2 * ROWS, DEEP),
        [VMEM] * 3,
        HBM,
        SPREAD,
        2 * 576 * WIDE * WIDE,
        6 << 20,
        [pltpu.VMEM((2, 2 * ROWS, DEEP), F32), pltpu.SemaphoreType.DMA((32,))],
    )(own, pair, jnp.asarray(column_source()))
    rows = lax.all_to_all(spread, ("y", "x", "core"), split_axis=0, concat_axis=0, tiled=True)

    row, col = call(
        shifts_kernel,
        "shifts",
        [shape(ROWS, 128), shape(1, OCC_WIN * VIRT)],
        [SMEM] * 5 + [VMEM],
        [VMEM] * 2,
        2,
        1,
        1 << 16,
    )(where, window_i, window_j, occupied_energy, virtual_energy, virtual_energy)
    high, low = call(
        place_kernel,
        "place",
        [shape(DEEP, WIDE, dtype=BF16)] * 2,
        [SMEM] + [VMEM] * 7,
        [VMEM] * 2,
        10,
        4 * DEEP * WIDE,
        8 * DEEP * WIDE,
    )(where, *shards)
    part, run_high, run_low = call(
        seven_kernel,
        "seven",
        [shape(2 * WIDE, WIDE)] + [shape(2 * WIDE, WIDE, dtype=BF16)] * 2,
        [SMEM, HBM] + [VMEM] * 2,
        [VMEM] * 3,
        24,
        12 * WIDE * WIDE * DEEP,
        12 * WIDE * DEEP,
        [pltpu.VMEM((2, 16, 2 * ROWS, DEEP), F32), pltpu.SemaphoreType.DMA((2, DEEP // STEP))],
    )(where, rows.reshape(16, 2, 2 * ROWS, DEEP), high, low)
    part, run_high, run_low, row, col = lax.optimization_barrier(
        (part, run_high, run_low, row, col)
    )
    def eighth(mine):
        return call(
            lambda *refs: eighth_kernel(mine, *refs),
            "eighth_mine" if mine else "eighth_theirs",
            shape(WIDE, WIDE),
            [SMEM] + [VMEM] * 4,
            VMEM,
            14,
            6 * WIDE * WIDE * WIDE,
            3 << 20,
            [pltpu.VMEM((WIDE, WIDE), BF16)] * 2,
        )(where, part, run_high, run_low, last)

    theirs = lax.ppermute(eighth(False), "core", swap)
    mine = eighth(True)
    packed = call(
        pack_kernel,
        "pack",
        shape(32, 3 * ROWS, 128),
        [SMEM] + [VMEM] * 2,
        VMEM,
        6,
        WIDE * WIDE,
        12 * WIDE * WIDE,
    )(where, mine, theirs)
    parts = lax.all_to_all(packed, ("zb", "y", "x"), split_axis=0, concat_axis=0, tiled=True)
    return call(
        divide_kernel,
        "divide",
        shape(ROWS, 16 * WIDE),
        [VMEM] * 3,
        VMEM,
        6,
        4 * ROWS * 16 * WIDE,
        1 << 20,
    )(parts, row, col)


def solution(mesh):
    fine = Mesh(mesh.devices.reshape(SIZES), AXES)
    split = P(AXES, None)
    return jax.shard_map(
        per_device,
        mesh=fine,
        in_specs=(split, split, P(), P(), P(), P()),
        out_specs=split,
        check_vma=False,
    )
```

```python
import jax
import jax.numpy as jnp
import numpy as np
from jax import lax
from jax.experimental import pallas as pl
from jax.experimental.pallas import tpu as pltpu
from jax.sharding import Mesh, PartitionSpec as P

AXES = ("zl4", "zb", "core", "y", "x", "zhi")
SIZES = (4, 2, 2, 4, 4, 2)
PLANE = ("y", "x")
VIRT = 1536
OCC_WIN = 4
ROWS = 12
WIDE = 384
SHARD = 16 * ROWS
DEEP = 8 * SHARD
STEP = 512
TALL = 62
SPREAD = 52
VMEM = pl.BlockSpec(memory_space=pltpu.VMEM)
SMEM = pl.BlockSpec(memory_space=pltpu.SMEM)
HBM = pl.BlockSpec(memory_space=pltpu.HBM)
F32 = jnp.float32
BF16 = jnp.bfloat16


def call(body, name, out, ins, outs, mib, flops, moved, scratch=()):
    return pl.pallas_call(
        body,
        out_shape=out,
        in_specs=ins,
        out_specs=outs,
        scratch_shapes=scratch,
        compiler_params=pltpu.CompilerParams(vmem_limit_bytes=mib * 1024 * 1024),
        cost_estimate=pl.CostEstimate(flops=flops, bytes_accessed=moved, transcendentals=0),
        name=name,
    )


def shape(*dims, dtype=F32):
    return jax.ShapeDtypeStruct(dims, dtype)


def column_source():
    return np.arange(WIDE, dtype=np.int32).reshape(16, 2, ROWS).transpose(1, 0, 2).reshape(1, WIDE)


def in_two(x):
    high = x.astype(BF16)
    return high, (x - high.astype(F32)).astype(BF16)


def run(copies):
    for copy in copies:
        copy.start()
    for copy in copies:
        copy.wait()


def halves_kernel(where_ref, a_ref, own_ref, other_ref, sems):
    zb = where_ref[0]
    copies = []
    for z in range(4):
        at = slice(768 * z, 768 * z + 768)
        far = pl.ds(pl.multiple_of(1536 * z + 768 - 768 * zb, 128), 768)
        near = pl.ds(pl.multiple_of(1536 * z + 768 * zb, 128), 768)
        copies.append(pltpu.make_async_copy(a_ref.at[:, far], other_ref.at[:, at], sems.at[z]))
        copies.append(pltpu.make_async_copy(a_ref.at[:, near], own_ref.at[:, at], sems.at[4 + z]))
    run(copies)


def blocks_kernel(b_ref, out_ref, sems):
    run(
        [
            pltpu.make_async_copy(
                b_ref.at[:, WIDE * i : WIDE * i + WIDE], out_ref.at[i], sems.at[i]
            )
            for i in range(16)
        ]
    )


def stack_kernel(blocks_ref, out_ref):
    for i in range(16):
        out_ref[ROWS * i : ROWS * i + ROWS, :] = blocks_ref[i]


def half_kernel(lower, x_ref, out_ref):
    out_ref[...] = x_ref[SHARD // 2 :, :] if lower else x_ref[: SHARD // 2, :]


def spread_kernel(own_ref, pair_ref, source_ref, out_ref, rows_ref, sems):
    x = jnp.concatenate([own_ref[...], pair_ref[...]], axis=0)
    wanted = lax.broadcasted_iota(jnp.int32, (WIDE, WIDE), 0) == source_ref[...]
    order = jnp.where(wanted, 1.0, 0.0).astype(BF16)
    copies = []
    for core in range(2):
        rest = jnp.concatenate(
            [x[:, 768 * z + WIDE * core : 768 * z + WIDE * core + WIDE] for z in range(4)], axis=0
        )
        total = None
        for _ in range(3):
            part = rest.astype(BF16)
            rest = rest - part.astype(F32)
            moved = jnp.dot(part, order, preferred_element_type=F32)
            total = moved if total is None else total + moved
        for z in range(4):
            rows_ref[core, :, WIDE * z : WIDE * z + WIDE] = total[24 * z : 24 * z + 24]
        for i in range(core, 32, 2):
            copies.append(pltpu.make_async_copy(rows_ref.at[core], out_ref.at[i], sems.at[i]))
            copies[-1].start()
    for copy in copies:
        copy.wait()


def block_of(ring, step):
    at = lax.rem(ring + 8 + step, 8)
    return lax.rem(at, 4), at // 4


def place_kernel(where_ref, *refs):
    shards, high_ref, low_ref = refs[:7], refs[7], refs[8]
    ring = where_ref[2]
    for shard, step in zip(shards, [0, -1, 1, -2, 2, -3, 3]):
        z, zhi = block_of(ring, step)
        at = pl.ds(pl.multiple_of((2 * z + zhi) * SHARD, 64), SHARD)
        high_ref[at, :], low_ref[at, :] = in_two(shard[...])
    z, zhi = block_of(ring, 4)
    at = pl.ds(pl.multiple_of((2 * z + zhi) * SHARD, 64), SHARD)
    high_ref[at, :] = jnp.zeros((SHARD, WIDE), BF16)
    low_ref[at, :] = jnp.zeros((SHARD, WIDE), BF16)


def seven_kernel(where_ref, rows_ref, high_ref, low_ref, part_ref, run_high_ref, run_low_ref, left_ref, sems):
    copies = []
    for k in range(DEEP // STEP):
        at = pl.ds(STEP * k, STEP)
        for core in range(2):
            which = 1 - where_ref[1] if core else where_ref[1]
            source = rows_ref.at[:, which, :, at]
            copies.append(pltpu.make_async_copy(source, left_ref.at[core, :, :, at], sems.at[core, k]))
            copies[-1].start()
    for k in range(DEEP // STEP):
        copies[2 * k].wait()
        copies[2 * k + 1].wait()
        at = slice(STEP * k, STEP * k + STEP)
        a_high, a_low = in_two(left_ref[:, :, :, at].reshape(2 * WIDE, STEP))
        b_high, b_low = high_ref[at, :], low_ref[at, :]
        term = jnp.dot(
            jnp.concatenate([a_high, a_low, a_high], axis=1),
            jnp.concatenate([b_high, b_high, b_low], axis=0),
            preferred_element_type=F32,
        )
        if k == 0:
            part_ref[...] = term
        else:
            part_ref[...] += term
    z, _ = block_of(where_ref[2], 4)
    last = left_ref[:, :, :, pl.ds(pl.multiple_of(z * WIDE, 128), WIDE)]
    run_high_ref[...], run_low_ref[...] = in_two(last.reshape(2 * WIDE, WIDE))


def eighth_kernel(mine, where_ref, part_ref, a_high_ref, a_low_ref, last_ref, out_ref, high_ref, low_ref):
    _, zhi = block_of(where_ref[2], 4)
    high_ref[...] = jnp.zeros((WIDE, WIDE), BF16)
    low_ref[...] = jnp.zeros((WIDE, WIDE), BF16)
    at = pl.ds(pl.multiple_of(zhi * SHARD, 64), SHARD)
    high_ref[at, :], low_ref[at, :] = in_two(last_ref[...])
    rows = slice(0, WIDE) if mine else slice(WIDE, 2 * WIDE)
    a_high, a_low, b_high, b_low = a_high_ref[rows, :], a_low_ref[rows, :], high_ref[...], low_ref[...]
    out_ref[...] = part_ref[rows, :] + jnp.dot(
        jnp.concatenate([a_high, a_low, a_high], axis=1),
        jnp.concatenate([b_high, b_high, b_low], axis=0),
        preferred_element_type=F32,
    )


def pack_kernel(where_ref, own_ref, other_ref, out_ref):
    for pair in range(2):
        zb = 1 - where_ref[0] if pair else where_ref[0]
        for i in range(16):
            rows = slice(24 * i + ROWS * pair, 24 * i + ROWS * pair + ROWS)
            total = own_ref[rows, :] + other_ref[rows, :]
            for g in range(3):
                at = slice(ROWS * g, ROWS * g + ROWS)
                out_ref[16 * zb + i, at, :] = total[:, 128 * g : 128 * g + 128]


def shifts_kernel(where_ref, wi_ref, wj_ref, occ_ref, virt_ref, lanes_ref, row_ref, col_ref):
    place = where_ref[3]
    per_orbital = VIRT // ROWS
    occ_i = occ_ref[wi_ref[place // per_orbital]]
    start = lax.rem(place, per_orbital) * ROWS
    at = lax.broadcasted_iota(jnp.int32, (ROWS, 128), 0)
    row = jnp.zeros((ROWS, 128), F32)
    for r in range(ROWS):
        row = jnp.where(at == r, occ_i - virt_ref[start + r], row)
    row_ref[...] = row
    for j in range(OCC_WIN):
        col_ref[:, VIRT * j : VIRT * j + VIRT] = occ_ref[wj_ref[j]] - lanes_ref[...].reshape(1, VIRT)


def divide_kernel(parts_ref, row_ref, col_ref, out_ref):
    row = row_ref[...]
    for i in range(16):
        for g in range(3):
            at = slice(ROWS * g, ROWS * g + ROWS)
            lanes = slice(WIDE * i + 128 * g, WIDE * i + 128 * g + 128)
            cycle = parts_ref[i, at, :] + parts_ref[16 + i, at, :]
            out_ref[:, lanes] = cycle / (row + col_ref[:, lanes])


def turn(x, step):
    index = lambda a: (a % 8 % 4) * 2 + a % 8 // 4
    return lax.ppermute(x, ("zl4", "zhi"), [(index(a), index(a + step)) for a in range(8)])


def per_device(amplitudes, integrals, occupied_energy, virtual_energy, window_i, window_j):
    swap = [(0, 1), (1, 0)]
    axis = lax.axis_index
    where = jnp.stack([axis("zb"), axis("core"), axis("zhi") * 4 + axis("zl4"), axis(AXES)])
    own, pair = call(
        halves_kernel,
        "halves",
        [shape(ROWS, 3072)] * 2,
        [SMEM, HBM],
        [VMEM] * 2,
        4,
        1,
        1 << 20,
        [pltpu.SemaphoreType.DMA((8,))],
    )(where, amplitudes)
    pair = lax.ppermute(pair, "zb", swap)
    blocks = call(
        blocks_kernel,
        "blocks",
        shape(16, ROWS, WIDE),
        [HBM],
        VMEM,
        TALL,
        1,
        1 << 20,
        [pltpu.SemaphoreType.DMA((16,))],
    )(integrals)
    blocks = lax.all_to_all(blocks, PLANE, split_axis=0, concat_axis=0, tiled=True)
    shard = call(
        stack_kernel,
        "stack",
        shape(SHARD, WIDE),
        [VMEM],
        VMEM,
        4,
        1,
        1 << 20,
    )(blocks)

    shards, right, left = [shard], shard, shard
    for _ in range(3):
        right, left = turn(right, 1), turn(left, -1)
        shards += [right, left]
    last = turn(right, 1)


    spread = call(
        spread_kernel,
        "spread",
        shape(32, 2 * ROWS, DEEP),
        [VMEM] * 3,
        HBM,
        SPREAD,
        2 * 576 * WIDE * WIDE,
        6 << 20,
        [pltpu.VMEM((2, 2 * ROWS, DEEP), F32), pltpu.SemaphoreType.DMA((32,))],
    )(own, pair, jnp.asarray(column_source()))
    rows = lax.all_to_all(spread, ("y", "x", "core"), split_axis=0, concat_axis=0, tiled=True)

    row, col = call(
        shifts_kernel,
        "shifts",
        [shape(ROWS, 128), shape(1, OCC_WIN * VIRT)],
        [SMEM] * 5 + [VMEM],
        [VMEM] * 2,
        2,
        1,
        1 << 16,
    )(where, window_i, window_j, occupied_energy, virtual_energy, virtual_energy)
    high, low = call(
        place_kernel,
        "place",
        [shape(DEEP, WIDE, dtype=BF16)] * 2,
        [SMEM] + [VMEM] * 7,
        [VMEM] * 2,
        10,
        4 * DEEP * WIDE,
        8 * DEEP * WIDE,
    )(where, *shards)
    part, run_high, run_low = call(
        seven_kernel,
        "seven",
        [shape(2 * WIDE, WIDE)] + [shape(2 * WIDE, WIDE, dtype=BF16)] * 2,
        [SMEM, HBM] + [VMEM] * 2,
        [VMEM] * 3,
        24,
        12 * WIDE * WIDE * DEEP,
        12 * WIDE * DEEP,
        [pltpu.VMEM((2, 16, 2 * ROWS, DEEP), F32), pltpu.SemaphoreType.DMA((2, DEEP // STEP))],
    )(where, rows.reshape(16, 2, 2 * ROWS, DEEP), high, low)
    part, run_high, run_low, row, col = lax.optimization_barrier(
        (part, run_high, run_low, row, col)
    )
    def eighth(mine):
        return call(
            lambda *refs: eighth_kernel(mine, *refs),
            "eighth_mine" if mine else "eighth_theirs",
            shape(WIDE, WIDE),
            [SMEM] + [VMEM] * 4,
            VMEM,
            14,
            6 * WIDE * WIDE * WIDE,
            3 << 20,
            [pltpu.VMEM((WIDE, WIDE), BF16)] * 2,
        )(where, part, run_high, run_low, last)

    theirs = lax.ppermute(eighth(False), "core", swap)
    mine = eighth(True)
    packed = call(
        pack_kernel,
        "pack",
        shape(32, 3 * ROWS, 128),
        [SMEM] + [VMEM] * 2,
        VMEM,
        6,
        WIDE * WIDE,
        12 * WIDE * WIDE,
    )(where, mine, theirs)
    parts = lax.all_to_all(packed, ("zb", "y", "x"), split_axis=0, concat_axis=0, tiled=True)
    return call(
        divide_kernel,
        "divide",
        shape(ROWS, 16 * WIDE),
        [VMEM] * 3,
        VMEM,
        6,
        4 * ROWS * 16 * WIDE,
        1 << 20,
    )(parts, row, col)


def solution(mesh):
    fine = Mesh(mesh.devices.reshape(SIZES), AXES)
    split = P(AXES, None)
    return jax.shard_map(
        per_device,
        mesh=fine,
        in_specs=(split, split, P(), P(), P(), P()),
        out_specs=split,
        check_vma=False,
    )
```

```python
import jax
import jax.numpy as jnp
import numpy as np
from jax import lax
from jax.experimental import pallas as pl
from jax.experimental.pallas import tpu as pltpu
from jax.sharding import Mesh, PartitionSpec as P

AXES = ("zl4", "zb", "core", "y", "x", "zhi")
SIZES = (4, 2, 2, 4, 4, 2)
PLANE = ("y", "x")
VIRT = 1536
OCC_WIN = 4
ROWS = 12
WIDE = 384
SHARD = 16 * ROWS
DEEP = 8 * SHARD
STEP = 512
TALL = 62
SPREAD = 52
VMEM = pl.BlockSpec(memory_space=pltpu.VMEM)
SMEM = pl.BlockSpec(memory_space=pltpu.SMEM)
HBM = pl.BlockSpec(memory_space=pltpu.HBM)
F32 = jnp.float32
BF16 = jnp.bfloat16


def call(body, name, out, ins, outs, mib, flops, moved, scratch=()):
    return pl.pallas_call(
        body,
        out_shape=out,
        in_specs=ins,
        out_specs=outs,
        scratch_shapes=scratch,
        compiler_params=pltpu.CompilerParams(vmem_limit_bytes=mib * 1024 * 1024),
        cost_estimate=pl.CostEstimate(flops=flops, bytes_accessed=moved, transcendentals=0),
        name=name,
    )


def shape(*dims, dtype=F32):
    return jax.ShapeDtypeStruct(dims, dtype)


def column_source():
    return np.arange(WIDE, dtype=np.int32).reshape(16, 2, ROWS).transpose(1, 0, 2).reshape(1, WIDE)


def in_two(x):
    high = x.astype(BF16)
    return high, (x - high.astype(F32)).astype(BF16)


def run(copies):
    for copy in copies:
        copy.start()
    for copy in copies:
        copy.wait()


def halves_kernel(where_ref, a_ref, own_ref, other_ref, sems):
    zb = where_ref[0]
    copies = []
    for z in range(4):
        at = slice(768 * z, 768 * z + 768)
        far = pl.ds(pl.multiple_of(1536 * z + 768 - 768 * zb, 128), 768)
        near = pl.ds(pl.multiple_of(1536 * z + 768 * zb, 128), 768)
        copies.append(pltpu.make_async_copy(a_ref.at[:, far], other_ref.at[:, at], sems.at[z]))
        copies.append(pltpu.make_async_copy(a_ref.at[:, near], own_ref.at[:, at], sems.at[4 + z]))
    run(copies)


def blocks_kernel(b_ref, out_ref, sems):
    run(
        [
            pltpu.make_async_copy(
                b_ref.at[:, WIDE * i : WIDE * i + WIDE], out_ref.at[i], sems.at[i]
            )
            for i in range(16)
        ]
    )


def stack_kernel(blocks_ref, out_ref):
    for i in range(16):
        out_ref[ROWS * i : ROWS * i + ROWS, :] = blocks_ref[i]


def half_kernel(lower, x_ref, out_ref):
    out_ref[...] = x_ref[SHARD // 2 :, :] if lower else x_ref[: SHARD // 2, :]


def spread_kernel(own_ref, pair_ref, source_ref, out_ref, rows_ref, sems):
    x = jnp.concatenate([own_ref[...], pair_ref[...]], axis=0)
    wanted = lax.broadcasted_iota(jnp.int32, (WIDE, WIDE), 0) == source_ref[...]
    order = jnp.where(wanted, 1.0, 0.0).astype(BF16)
    copies = []
    for core in range(2):
        rest = jnp.concatenate(
            [x[:, 768 * z + WIDE * core : 768 * z + WIDE * core + WIDE] for z in range(4)], axis=0
        )
        total = None
        for _ in range(3):
            part = rest.astype(BF16)
            rest = rest - part.astype(F32)
            moved = jnp.dot(part, order, preferred_element_type=F32)
            total = moved if total is None else total + moved
        for z in range(4):
            rows_ref[core, :, WIDE * z : WIDE * z + WIDE] = total[24 * z : 24 * z + 24]
        for i in range(core, 32, 2):
            copies.append(pltpu.make_async_copy(rows_ref.at[core], out_ref.at[i], sems.at[i]))
            copies[-1].start()
    for copy in copies:
        copy.wait()


def product(a_high, a_low, b_high, b_low):
    dot = lambda a, b: jnp.dot(a, b, preferred_element_type=F32)
    both = dot(a_high, jnp.concatenate([b_high, b_low], axis=1))
    return both[:, :WIDE] + (both[:, WIDE:] + dot(a_low, b_high))


def block_of(ring, step):
    at = lax.rem(ring + 8 + step, 8)
    return lax.rem(at, 4), at // 4


def place_kernel(where_ref, *refs):
    shards, high_ref, low_ref = refs[:7], refs[7], refs[8]
    ring = where_ref[2]
    for shard, step in zip(shards, [0, -1, 1, -2, 2, -3, 3]):
        z, zhi = block_of(ring, step)
        at = pl.ds(pl.multiple_of((2 * z + zhi) * SHARD, 64), SHARD)
        high_ref[at, :], low_ref[at, :] = in_two(shard[...])
    z, zhi = block_of(ring, 4)
    at = pl.ds(pl.multiple_of((2 * z + zhi) * SHARD, 64), SHARD)
    high_ref[at, :] = jnp.zeros((SHARD, WIDE), BF16)
    low_ref[at, :] = jnp.zeros((SHARD, WIDE), BF16)


def seven_kernel(where_ref, rows_ref, high_ref, low_ref, part_ref, run_high_ref, run_low_ref, left_ref, sems):
    copies = []
    for k in range(DEEP // STEP):
        at = pl.ds(STEP * k, STEP)
        for core in range(2):
            which = 1 - where_ref[1] if core else where_ref[1]
            source = rows_ref.at[:, which, :, at]
            copies.append(pltpu.make_async_copy(source, left_ref.at[core, :, :, at], sems.at[core, k]))
            copies[-1].start()
    for copy in copies:
        copy.wait()
    a_high, a_low = in_two(left_ref[...].reshape(2 * WIDE, DEEP))
    part_ref[...] = product(a_high, a_low, high_ref[...], low_ref[...])
    z, _ = block_of(where_ref[2], 4)
    last = left_ref[:, :, :, pl.ds(pl.multiple_of(z * WIDE, 128), WIDE)]
    run_high_ref[...], run_low_ref[...] = in_two(last.reshape(2 * WIDE, WIDE))


def eighth_kernel(mine, where_ref, part_ref, a_high_ref, a_low_ref, last_ref, out_ref, high_ref, low_ref):
    _, zhi = block_of(where_ref[2], 4)
    high_ref[...] = jnp.zeros((WIDE, WIDE), BF16)
    low_ref[...] = jnp.zeros((WIDE, WIDE), BF16)
    at = pl.ds(pl.multiple_of(zhi * SHARD, 64), SHARD)
    high_ref[at, :], low_ref[at, :] = in_two(last_ref[...])
    rows = slice(0, WIDE) if mine else slice(WIDE, 2 * WIDE)
    out_ref[...] = part_ref[rows, :] + product(
        a_high_ref[rows, :], a_low_ref[rows, :], high_ref[...], low_ref[...]
    )


def pack_kernel(where_ref, own_ref, other_ref, out_ref):
    for pair in range(2):
        zb = 1 - where_ref[0] if pair else where_ref[0]
        for i in range(16):
            rows = slice(24 * i + ROWS * pair, 24 * i + ROWS * pair + ROWS)
            total = own_ref[rows, :] + other_ref[rows, :]
            for g in range(3):
                at = slice(ROWS * g, ROWS * g + ROWS)
                out_ref[16 * zb + i, at, :] = total[:, 128 * g : 128 * g + 128]


def shifts_kernel(where_ref, wi_ref, wj_ref, occ_ref, virt_ref, lanes_ref, row_ref, col_ref):
    place = where_ref[3]
    per_orbital = VIRT // ROWS
    occ_i = occ_ref[wi_ref[place // per_orbital]]
    start = lax.rem(place, per_orbital) * ROWS
    at = lax.broadcasted_iota(jnp.int32, (ROWS, 128), 0)
    row = jnp.zeros((ROWS, 128), F32)
    for r in range(ROWS):
        row = jnp.where(at == r, occ_i - virt_ref[start + r], row)
    row_ref[...] = row
    for j in range(OCC_WIN):
        col_ref[:, VIRT * j : VIRT * j + VIRT] = occ_ref[wj_ref[j]] - lanes_ref[...].reshape(1, VIRT)


def divide_kernel(parts_ref, row_ref, col_ref, out_ref):
    row = row_ref[...]
    for i in range(16):
        for g in range(3):
            at = slice(ROWS * g, ROWS * g + ROWS)
            lanes = slice(WIDE * i + 128 * g, WIDE * i + 128 * g + 128)
            cycle = parts_ref[i, at, :] + parts_ref[16 + i, at, :]
            out_ref[:, lanes] = cycle / (row + col_ref[:, lanes])


def turn(x, step):
    index = lambda a: (a % 8 % 4) * 2 + a % 8 // 4
    return lax.ppermute(x, ("zl4", "zhi"), [(index(a), index(a + step)) for a in range(8)])


def per_device(amplitudes, integrals, occupied_energy, virtual_energy, window_i, window_j):
    swap = [(0, 1), (1, 0)]
    axis = lax.axis_index
    where = jnp.stack([axis("zb"), axis("core"), axis("zhi") * 4 + axis("zl4"), axis(AXES)])
    own, pair = call(
        halves_kernel,
        "halves",
        [shape(ROWS, 3072)] * 2,
        [SMEM, HBM],
        [VMEM] * 2,
        4,
        1,
        1 << 20,
        [pltpu.SemaphoreType.DMA((8,))],
    )(where, amplitudes)
    pair = lax.ppermute(pair, "zb", swap)
    blocks = call(
        blocks_kernel,
        "blocks",
        shape(16, ROWS, WIDE),
        [HBM],
        VMEM,
        TALL,
        1,
        1 << 20,
        [pltpu.SemaphoreType.DMA((16,))],
    )(integrals)
    blocks = lax.all_to_all(blocks, PLANE, split_axis=0, concat_axis=0, tiled=True)
    shard = call(
        stack_kernel,
        "stack",
        shape(SHARD, WIDE),
        [VMEM],
        VMEM,
        4,
        1,
        1 << 20,
    )(blocks)

    shards, right, left = [shard], shard, shard
    for _ in range(3):
        right, left = turn(right, 1), turn(left, -1)
        shards += [right, left]
    last = turn(right, 1)


    spread = call(
        spread_kernel,
        "spread",
        shape(32, 2 * ROWS, DEEP),
        [VMEM] * 3,
        HBM,
        SPREAD,
        2 * 576 * WIDE * WIDE,
        6 << 20,
        [pltpu.VMEM((2, 2 * ROWS, DEEP), F32), pltpu.SemaphoreType.DMA((32,))],
    )(own, pair, jnp.asarray(column_source()))
    rows = lax.all_to_all(spread, ("y", "x", "core"), split_axis=0, concat_axis=0, tiled=True)

    row, col = call(
        shifts_kernel,
        "shifts",
        [shape(ROWS, 128), shape(1, OCC_WIN * VIRT)],
        [SMEM] * 5 + [VMEM],
        [VMEM] * 2,
        2,
        1,
        1 << 16,
    )(where, window_i, window_j, occupied_energy, virtual_energy, virtual_energy)
    high, low = call(
        place_kernel,
        "place",
        [shape(DEEP, WIDE, dtype=BF16)] * 2,
        [SMEM] + [VMEM] * 7,
        [VMEM] * 2,
        10,
        4 * DEEP * WIDE,
        8 * DEEP * WIDE,
    )(where, *shards)
    part, run_high, run_low = call(
        seven_kernel,
        "seven",
        [shape(2 * WIDE, WIDE)] + [shape(2 * WIDE, WIDE, dtype=BF16)] * 2,
        [SMEM, HBM] + [VMEM] * 2,
        [VMEM] * 3,
        24,
        12 * WIDE * WIDE * DEEP,
        12 * WIDE * DEEP,
        [pltpu.VMEM((2, 16, 2 * ROWS, DEEP), F32), pltpu.SemaphoreType.DMA((2, DEEP // STEP))],
    )(where, rows.reshape(16, 2, 2 * ROWS, DEEP), high, low)
    part, run_high, run_low, row, col = lax.optimization_barrier(
        (part, run_high, run_low, row, col)
    )
    def eighth(mine):
        return call(
            lambda *refs: eighth_kernel(mine, *refs),
            "eighth_mine" if mine else "eighth_theirs",
            shape(WIDE, WIDE),
            [SMEM] + [VMEM] * 4,
            VMEM,
            14,
            6 * WIDE * WIDE * WIDE,
            3 << 20,
            [pltpu.VMEM((WIDE, WIDE), BF16)] * 2,
        )(where, part, run_high, run_low, last)

    theirs = lax.ppermute(eighth(False), "core", swap)
    mine = eighth(True)
    packed = call(
        pack_kernel,
        "pack",
        shape(32, 3 * ROWS, 128),
        [SMEM] + [VMEM] * 2,
        VMEM,
        6,
        WIDE * WIDE,
        12 * WIDE * WIDE,
    )(where, mine, theirs)
    parts = lax.all_to_all(packed, ("zb", "y", "x"), split_axis=0, concat_axis=0, tiled=True)
    return call(
        divide_kernel,
        "divide",
        shape(ROWS, 16 * WIDE),
        [VMEM] * 3,
        VMEM,
        6,
        4 * ROWS * 16 * WIDE,
        1 << 20,
    )(parts, row, col)


def solution(mesh):
    fine = Mesh(mesh.devices.reshape(SIZES), AXES)
    split = P(AXES, None)
    return jax.shard_map(
        per_device,
        mesh=fine,
        in_specs=(split, split, P(), P(), P(), P()),
        out_specs=split,
        check_vma=False,
    )
```

```python
import jax
import jax.numpy as jnp
import numpy as np
from jax import lax
from jax.experimental import pallas as pl
from jax.experimental.pallas import tpu as pltpu
from jax.sharding import Mesh, PartitionSpec as P

AXES = ("zl4", "zb", "core", "y", "x", "zhi")
SIZES = (4, 2, 2, 4, 4, 2)
PLANE = ("y", "x")
VIRT = 1536
OCC_WIN = 4
ROWS = 12
WIDE = 384
SHARD = 16 * ROWS
DEEP = 8 * SHARD
STEP = 512
TALL = 62
SPREAD = 52
VMEM = pl.BlockSpec(memory_space=pltpu.VMEM)
SMEM = pl.BlockSpec(memory_space=pltpu.SMEM)
HBM = pl.BlockSpec(memory_space=pltpu.HBM)
F32 = jnp.float32
BF16 = jnp.bfloat16


def call(body, name, out, ins, outs, mib, flops, moved, scratch=()):
    return pl.pallas_call(
        body,
        out_shape=out,
        in_specs=ins,
        out_specs=outs,
        scratch_shapes=scratch,
        compiler_params=pltpu.CompilerParams(vmem_limit_bytes=mib * 1024 * 1024),
        cost_estimate=pl.CostEstimate(flops=flops, bytes_accessed=moved, transcendentals=0),
        name=name,
    )


def shape(*dims, dtype=F32):
    return jax.ShapeDtypeStruct(dims, dtype)


def column_source():
    return np.arange(WIDE, dtype=np.int32).reshape(16, 2, ROWS).transpose(1, 0, 2).reshape(1, WIDE)


def in_two(x):
    high = x.astype(BF16)
    return high, (x - high.astype(F32)).astype(BF16)


def run(copies):
    for copy in copies:
        copy.start()
    for copy in copies:
        copy.wait()


def halves_kernel(where_ref, a_ref, own_ref, other_ref, sems):
    zb = where_ref[0]
    copies = []
    for z in range(4):
        at = slice(768 * z, 768 * z + 768)
        far = pl.ds(pl.multiple_of(1536 * z + 768 - 768 * zb, 128), 768)
        near = pl.ds(pl.multiple_of(1536 * z + 768 * zb, 128), 768)
        copies.append(pltpu.make_async_copy(a_ref.at[:, far], other_ref.at[:, at], sems.at[z]))
        copies.append(pltpu.make_async_copy(a_ref.at[:, near], own_ref.at[:, at], sems.at[4 + z]))
    run(copies)


def blocks_kernel(b_ref, out_ref, sems):
    run(
        [
            pltpu.make_async_copy(
                b_ref.at[:, WIDE * i : WIDE * i + WIDE], out_ref.at[i], sems.at[i]
            )
            for i in range(16)
        ]
    )


def stack_kernel(blocks_ref, out_ref):
    for i in range(16):
        out_ref[ROWS * i : ROWS * i + ROWS, :] = blocks_ref[i]


def half_kernel(lower, x_ref, out_ref):
    out_ref[...] = x_ref[SHARD // 2 :, :] if lower else x_ref[: SHARD // 2, :]


def spread_kernel(own_ref, pair_ref, source_ref, out_ref, rows_ref, sems):
    x = jnp.concatenate([own_ref[...], pair_ref[...]], axis=0)
    wanted = lax.broadcasted_iota(jnp.int32, (WIDE, WIDE), 0) == source_ref[...]
    order = jnp.where(wanted, 1.0, 0.0).astype(BF16)
    copies = []
    for core in range(2):
        rest = jnp.concatenate(
            [x[:, 768 * z + WIDE * core : 768 * z + WIDE * core + WIDE] for z in range(4)], axis=0
        )
        total = None
        for _ in range(3):
            part = rest.astype(BF16)
            rest = rest - part.astype(F32)
            moved = jnp.dot(part, order, preferred_element_type=F32)
            total = moved if total is None else total + moved
        for z in range(4):
            rows_ref[core, :, WIDE * z : WIDE * z + WIDE] = total[24 * z : 24 * z + 24]
        for i in range(core, 32, 2):
            copies.append(pltpu.make_async_copy(rows_ref.at[core], out_ref.at[i], sems.at[i]))
            copies[-1].start()
    for copy in copies:
        copy.wait()


def block_of(ring, step):
    at = lax.rem(ring + 8 + step, 8)
    return lax.rem(at, 4), at // 4


def place_kernel(where_ref, *refs):
    shards, high_ref, low_ref = refs[:7], refs[7], refs[8]
    ring = where_ref[2]
    for shard, step in zip(shards, [0, -1, 1, -2, 2, -3, 3]):
        z, zhi = block_of(ring, step)
        at = pl.ds(pl.multiple_of((2 * z + zhi) * SHARD, 64), SHARD)
        high_ref[at, :], low_ref[at, :] = in_two(shard[...])
    z, zhi = block_of(ring, 4)
    at = pl.ds(pl.multiple_of((2 * z + zhi) * SHARD, 64), SHARD)
    high_ref[at, :] = jnp.zeros((SHARD, WIDE), BF16)
    low_ref[at, :] = jnp.zeros((SHARD, WIDE), BF16)


def seven_kernel(where_ref, rows_ref, high_ref, low_ref, part_ref, run_high_ref, run_low_ref, left_ref, sems):
    copies = []
    for k in range(DEEP // STEP):
        at = pl.ds(STEP * k, STEP)
        for core in range(2):
            which = 1 - where_ref[1] if core else where_ref[1]
            source = rows_ref.at[:, which, :, at]
            copies.append(pltpu.make_async_copy(source, left_ref.at[core, :, :, at], sems.at[core, k]))
            copies[-1].start()
    for k in range(DEEP // STEP):
        copies[2 * k].wait()
        copies[2 * k + 1].wait()
        at = slice(STEP * k, STEP * k + STEP)
        a_high, a_low = in_two(left_ref[:, :, :, at].reshape(2 * WIDE, STEP))
        b_high, b_low = high_ref[at, :], low_ref[at, :]
        term = jnp.dot(
            jnp.concatenate([a_high, a_low, a_high], axis=1),
            jnp.concatenate([b_high, b_high, b_low], axis=0),
            preferred_element_type=F32,
        )
        if k == 0:
            part_ref[...] = term
        else:
            part_ref[...] += term
    z, _ = block_of(where_ref[2], 4)
    last = left_ref[:, :, :, pl.ds(pl.multiple_of(z * WIDE, 128), WIDE)]
    run_high_ref[...], run_low_ref[...] = in_two(last.reshape(2 * WIDE, WIDE))


def eighth_kernel(mine, where_ref, part_ref, a_high_ref, a_low_ref, last_ref, out_ref, high_ref, low_ref):
    _, zhi = block_of(where_ref[2], 4)
    high_ref[...] = jnp.zeros((WIDE, WIDE), BF16)
    low_ref[...] = jnp.zeros((WIDE, WIDE), BF16)
    at = pl.ds(pl.multiple_of(zhi * SHARD, 64), SHARD)
    high_ref[at, :], low_ref[at, :] = in_two(last_ref[...])
    rows = slice(0, WIDE) if mine else slice(WIDE, 2 * WIDE)
    a_high, a_low, b_high, b_low = a_high_ref[rows, :], a_low_ref[rows, :], high_ref[...], low_ref[...]
    out_ref[...] = part_ref[rows, :] + jnp.dot(
        jnp.concatenate([a_high, a_low, a_high], axis=1),
        jnp.concatenate([b_high, b_high, b_low], axis=0),
        preferred_element_type=F32,
    )


def pack_kernel(where_ref, own_ref, other_ref, out_ref):
    for pair in range(2):
        zb = 1 - where_ref[0] if pair else where_ref[0]
        for i in range(16):
            rows = slice(24 * i + ROWS * pair, 24 * i + ROWS * pair + ROWS)
            total = own_ref[rows, :] + other_ref[rows, :]
            for g in range(3):
                at = slice(ROWS * g, ROWS * g + ROWS)
                out_ref[16 * zb + i % 4 * 4 + i // 4, at, :] = total[:, 128 * g : 128 * g + 128]


def shifts_kernel(where_ref, wi_ref, wj_ref, occ_ref, virt_ref, lanes_ref, row_ref, col_ref):
    place = where_ref[3]
    per_orbital = VIRT // ROWS
    occ_i = occ_ref[wi_ref[place // per_orbital]]
    start = lax.rem(place, per_orbital) * ROWS
    at = lax.broadcasted_iota(jnp.int32, (ROWS, 128), 0)
    row = jnp.zeros((ROWS, 128), F32)
    for r in range(ROWS):
        row = jnp.where(at == r, occ_i - virt_ref[start + r], row)
    row_ref[...] = row
    for j in range(OCC_WIN):
        col_ref[:, VIRT * j : VIRT * j + VIRT] = occ_ref[wj_ref[j]] - lanes_ref[...].reshape(1, VIRT)


def divide_kernel(parts_ref, row_ref, col_ref, out_ref):
    row = row_ref[...]
    for i in range(16):
        for g in range(3):
            at = slice(ROWS * g, ROWS * g + ROWS)
            lanes = slice(WIDE * i + 128 * g, WIDE * i + 128 * g + 128)
            cycle = parts_ref[i, at, :] + parts_ref[16 + i, at, :]
            out_ref[:, lanes] = cycle / (row + col_ref[:, lanes])


def turn(x, step):
    index = lambda a: (a % 8 % 4) * 2 + a % 8 // 4
    return lax.ppermute(x, ("zl4", "zhi"), [(index(a), index(a + step)) for a in range(8)])


def per_device(amplitudes, integrals, occupied_energy, virtual_energy, window_i, window_j):
    swap = [(0, 1), (1, 0)]
    axis = lax.axis_index
    where = jnp.stack([axis("zb"), axis("core"), axis("zhi") * 4 + axis("zl4"), axis(AXES)])
    own, pair = call(
        halves_kernel,
        "halves",
        [shape(ROWS, 3072)] * 2,
        [SMEM, HBM],
        [VMEM] * 2,
        4,
        1,
        1 << 20,
        [pltpu.SemaphoreType.DMA((8,))],
    )(where, amplitudes)
    pair = lax.ppermute(pair, "zb", swap)
    blocks = call(
        blocks_kernel,
        "blocks",
        shape(16, ROWS, WIDE),
        [HBM],
        VMEM,
        TALL,
        1,
        1 << 20,
        [pltpu.SemaphoreType.DMA((16,))],
    )(integrals)
    blocks = lax.all_to_all(blocks, PLANE, split_axis=0, concat_axis=0, tiled=True)
    shard = call(
        stack_kernel,
        "stack",
        shape(SHARD, WIDE),
        [VMEM],
        VMEM,
        4,
        1,
        1 << 20,
    )(blocks)

    shards, right, left = [shard], shard, shard
    for _ in range(3):
        right, left = turn(right, 1), turn(left, -1)
        shards += [right, left]
    last = turn(right, 1)


    spread = call(
        spread_kernel,
        "spread",
        shape(32, 2 * ROWS, DEEP),
        [VMEM] * 3,
        HBM,
        SPREAD,
        2 * 576 * WIDE * WIDE,
        6 << 20,
        [pltpu.VMEM((2, 2 * ROWS, DEEP), F32), pltpu.SemaphoreType.DMA((32,))],
    )(own, pair, jnp.asarray(column_source()))
    rows = lax.all_to_all(spread, ("x", "y", "core"), split_axis=0, concat_axis=0, tiled=True)

    row, col = call(
        shifts_kernel,
        "shifts",
        [shape(ROWS, 128), shape(1, OCC_WIN * VIRT)],
        [SMEM] * 5 + [VMEM],
        [VMEM] * 2,
        2,
        1,
        1 << 16,
    )(where, window_i, window_j, occupied_energy, virtual_energy, virtual_energy)
    high, low = call(
        place_kernel,
        "place",
        [shape(DEEP, WIDE, dtype=BF16)] * 2,
        [SMEM] + [VMEM] * 7,
        [VMEM] * 2,
        10,
        4 * DEEP * WIDE,
        8 * DEEP * WIDE,
    )(where, *shards)
    part, run_high, run_low = call(
        seven_kernel,
        "seven",
        [shape(2 * WIDE, WIDE)] + [shape(2 * WIDE, WIDE, dtype=BF16)] * 2,
        [SMEM, HBM] + [VMEM] * 2,
        [VMEM] * 3,
        24,
        12 * WIDE * WIDE * DEEP,
        12 * WIDE * DEEP,
        [pltpu.VMEM((2, 16, 2 * ROWS, DEEP), F32), pltpu.SemaphoreType.DMA((2, DEEP // STEP))],
    )(where, rows.reshape(16, 2, 2 * ROWS, DEEP), high, low)
    part, run_high, run_low, row, col = lax.optimization_barrier(
        (part, run_high, run_low, row, col)
    )
    def eighth(mine):
        return call(
            lambda *refs: eighth_kernel(mine, *refs),
            "eighth_mine" if mine else "eighth_theirs",
            shape(WIDE, WIDE),
            [SMEM] + [VMEM] * 4,
            VMEM,
            14,
            6 * WIDE * WIDE * WIDE,
            3 << 20,
            [pltpu.VMEM((WIDE, WIDE), BF16)] * 2,
        )(where, part, run_high, run_low, last)

    theirs = lax.ppermute(eighth(False), "core", swap)
    mine = eighth(True)
    packed = call(
        pack_kernel,
        "pack",
        shape(32, 3 * ROWS, 128),
        [SMEM] + [VMEM] * 2,
        VMEM,
        6,
        WIDE * WIDE,
        12 * WIDE * WIDE,
    )(where, mine, theirs)
    parts = lax.all_to_all(packed, ("zb", "y", "x"), split_axis=0, concat_axis=0, tiled=True)
    return call(
        divide_kernel,
        "divide",
        shape(ROWS, 16 * WIDE),
        [VMEM] * 3,
        VMEM,
        6,
        4 * ROWS * 16 * WIDE,
        1 << 20,
    )(parts, row, col)


def solution(mesh):
    fine = Mesh(mesh.devices.reshape(SIZES), AXES)
    split = P(AXES, None)
    return jax.shard_map(
        per_device,
        mesh=fine,
        in_specs=(split, split, P(), P(), P(), P()),
        out_specs=split,
        check_vma=False,
    )
```
